256 devices in a mesh: trk: 64 (over x, z, core), frm: 4 (over y).
Axes of the slice: x: 4, y: 4, z: 8, core: 2. Of those that a mesh axis runs over, the one named last changes fastest.
Arguments:
- tokens: bfloat16 [2048, 32, 384], P('trk', 'frm'), may hold values from -10 to 10
- visible: int32 [2048, 32], P('trk', 'frm'), may hold values from 0 to 1, as said below
- virtual: bfloat16 [64, 32, 384], P(None, 'frm'), may hold values from -10 to 10
- time_qkv: bfloat16 [384, 1152], replicated, may hold values from -2 to 2
- time_out: bfloat16 [384, 384], replicated, may hold values from -0.3125 to 0.3125
- virt_q: bfloat16 [384, 384], replicated, may hold values from -2 to 2
- virt_kv: bfloat16 [384, 768], replicated, may hold values from -2 to 2
- virt_out: bfloat16 [384, 384], replicated, may hold values from -0.3125 to 0.3125
- self_qkv: bfloat16 [384, 1152], replicated, may hold values from -2 to 2
- self_out: bfloat16 [384, 384], replicated, may hold values from -0.3125 to 0.3125
- back_q: bfloat16 [384, 384], replicated, may hold values from -2 to 2
- back_kv: bfloat16 [384, 768], replicated, may hold values from -2 to 2
- back_out: bfloat16 [384, 384], replicated, may hold values from -0.3125 to 0.3125
Outputs:
- tracks_out: bfloat16 [2048, 32, 384], P('trk', 'frm')
- virtual_out: bfloat16 [64, 32, 384], P(None, 'frm')
The draws below stay inside these ranges and needn't reach their ends.
Inputs may be any that keep to these rules, and one draw needn't show every extreme that they name: 1 where the track is visible in the frame, else 0; in every frame at least one track is visible.
All inputs are finite; a program needn't handle non-finite values.
Results may differ from the reference program's by a relative error of at most 0.015.
Values may be sent and summed in bfloat16 or wider, within the bound.
No kernel may reach another device: no remote copies, remote signals or barrier semaphores. Data moves between devices by JAX's collectives and lax.ppermute only.
A program may use at most 384 MiB of HBM per device.

```python
import math
import jax
import jax.numpy as jnp
from jax import lax

D = 384
HEADS = 8
VIRT = 64
FRAMES = 32
TRACKS = 2048


def drawn_weight(key, row_count, col_count):
    return jnp.clip(jax.random.normal(key, (row_count, col_count), jnp.float32), -6.0, 6.0) * D ** (-0.5)


def draw_tokens(key, part):
    key = jax.random.fold_in(key, 21)
    first = jax.random.fold_in(key, 0)
    shape_all = (TRACKS, FRAMES, D)
    values = jnp.clip(jax.random.normal(first, shape_all, jnp.float32), -6.0, 6.0)
    return values.astype(jnp.bfloat16)


def draw_virtual(key, part):
    key = jax.random.fold_in(key, 23)
    first = jax.random.fold_in(key, 0)
    shape_all = (VIRT, FRAMES, D)
    values = jnp.clip(jax.random.normal(first, shape_all, jnp.float32), -6.0, 6.0)
    return values.astype(jnp.bfloat16)


def draw_visible(key, part):
    key = jax.random.fold_in(key, 31)
    first, second = jax.random.split(key, 2)
    seen_draw = jax.random.randint(first, (TRACKS, FRAMES), 0, 4) < 3
    picked = jax.random.randint(second, (FRAMES,), 0, TRACKS)
    forced = jnp.arange(TRACKS)[:, None] == picked[None, :]
    return jnp.logical_or(seen_draw, forced).astype(jnp.int32)


def draw_time_qkv(key, part):
    key = jax.random.fold_in(key, 41)
    matrix = drawn_weight(key, D, 3 * D)
    return matrix.astype(jnp.bfloat16)


def draw_virt_q(key, part):
    key = jax.random.fold_in(key, 43)
    matrix = drawn_weight(key, D, D)
    return matrix.astype(jnp.bfloat16)


def draw_virt_kv(key, part):
    key = jax.random.fold_in(key, 47)
    matrix = drawn_weight(key, D, 2 * D)
    return matrix.astype(jnp.bfloat16)


def draw_self_qkv(key, part):
    key = jax.random.fold_in(key, 53)
    matrix = drawn_weight(key, D, 3 * D)
    return matrix.astype(jnp.bfloat16)


def draw_back_q(key, part):
    key = jax.random.fold_in(key, 59)
    matrix = drawn_weight(key, D, D)
    return matrix.astype(jnp.bfloat16)


def draw_back_kv(key, part):
    key = jax.random.fold_in(key, 61)
    matrix = drawn_weight(key, D, 2 * D)
    return matrix.astype(jnp.bfloat16)


def gaussian(rng, dims, width, limit, held_as=jnp.bfloat16):
    entries = width * jax.random.normal(rng, dims, jnp.float32)
    return jnp.clip(entries, min=-limit, max=limit).astype(held_as)


def setup_inputs(seed: int = 0) -> dict:
    streams_of = jax.random.split(jax.random.key(seed), 14)
    tokens = draw_tokens(jax.random.fold_in(streams_of[13], 71), 0)
    visible = draw_visible(jax.random.fold_in(streams_of[13], 71), 0)
    virtual = draw_virtual(jax.random.fold_in(streams_of[13], 71), 0)
    time_qkv = draw_time_qkv(jax.random.fold_in(streams_of[13], 71), 0)
    time_out = gaussian(streams_of[4], (D, D), D ** -0.5, 0.3125)
    virt_q = draw_virt_q(jax.random.fold_in(streams_of[13], 71), 0)
    virt_kv = draw_virt_kv(jax.random.fold_in(streams_of[13], 71), 0)
    virt_out = gaussian(streams_of[7], (D, D), D ** -0.5, 0.3125)
    self_qkv = draw_self_qkv(jax.random.fold_in(streams_of[13], 71), 0)
    self_out = gaussian(streams_of[9], (D, D), D ** -0.5, 0.3125)
    back_q = draw_back_q(jax.random.fold_in(streams_of[13], 71), 0)
    back_kv = draw_back_kv(jax.random.fold_in(streams_of[13], 71), 0)
    back_out = gaussian(streams_of[12], (D, D), D ** -0.5, 0.3125)
    return dict(tokens=tokens, visible=visible, virtual=virtual, time_qkv=time_qkv, time_out=time_out, virt_q=virt_q, virt_kv=virt_kv, virt_out=virt_out, self_qkv=self_qkv, self_out=self_out, back_q=back_q, back_kv=back_kv, back_out=back_out)


EPS = 1e-05
NEG = -1e+30

def normalize(values):
    widened = values.astype(jnp.float32)
    center = lax.optimization_barrier(jnp.mean(widened, -1, keepdims=True))
    shifted = widened - center
    return (shifted * lax.rsqrt(lax.optimization_barrier(jnp.mean(shifted * shifted, -1, keepdims=True)) + EPS)).astype(jnp.bfloat16)

def project(values, weight):
    leading = values.shape[:-1]
    flat = values.reshape(-1, values.shape[-1])
    return jnp.dot(flat, weight, preferred_element_type=jnp.float32).reshape(leading + (weight.shape[1],))

def split_heads(values):
    return values.reshape(values.shape[:-1] + (HEADS, values.shape[-1] // HEADS))

def time_block(rows_in, time_qkv, time_out):
    scaling = (D // HEADS) ** (-0.5)
    projected = project(normalize(rows_in), time_qkv).astype(jnp.bfloat16)
    queries = split_heads(projected[..., :D]).astype(jnp.float32)
    keys_all = split_heads(projected[..., D:2 * D]).astype(jnp.float32)
    values_all = split_heads(projected[..., 2 * D:]).astype(jnp.float32)
    scores = jnp.einsum('bthe,bshe->bhts', queries, keys_all) * scaling
    weights = jax.nn.softmax(scores, -1).astype(jnp.bfloat16)
    mixed = jnp.einsum('bhts,bshe->bthe', weights.astype(jnp.float32), values_all).astype(jnp.bfloat16)
    mixed = mixed.reshape(rows_in.shape)
    return (rows_in.astype(jnp.float32) + project(mixed, time_out)).astype(jnp.bfloat16)

def virtual_self(virt_cross, self_qkv, self_out):
    scaling = (D // HEADS) ** (-0.5)
    self_proj = project(normalize(virt_cross), self_qkv).astype(jnp.bfloat16)
    self_query = split_heads(self_proj[..., :D]).astype(jnp.float32)
    self_keys = split_heads(self_proj[..., D:2 * D]).astype(jnp.float32)
    self_values = split_heads(self_proj[..., 2 * D:]).astype(jnp.float32)
    scores = jnp.einsum('ifhe,jfhe->fhij', self_query, self_keys) * scaling
    self_weights = jax.nn.softmax(scores, -1).astype(jnp.bfloat16)
    self_mixed = jnp.einsum('fhij,jfhe->ifhe', self_weights.astype(jnp.float32), self_values).astype(jnp.bfloat16)
    self_mixed = self_mixed.reshape(virt_cross.shape)
    return (virt_cross.astype(jnp.float32) + project(self_mixed, self_out)).astype(jnp.bfloat16)

def reference(tokens, visible, virtual, time_qkv, time_out, virt_q, virt_kv, virt_out, self_qkv, self_out, back_q, back_kv, back_out):
    scaling = (D // HEADS) ** (-0.5)
    number = tokens.shape[0]
    length = math.gcd(number, 512)
    blocked = tokens.reshape(number // length, length, FRAMES, D)
    updated = lax.map(lambda block_rows: time_block(block_rows, time_qkv, time_out), blocked)
    seen_blocks = visible.reshape(number // length, length, FRAMES)
    virt_norm = normalize(virtual)
    virt_query = split_heads(project(virt_norm, virt_q).astype(jnp.bfloat16)).astype(jnp.float32)

    def absorb(carry, pieces):
        running_peak, denominator, weighted = carry
        track_rows, seen_now = pieces
        key_value = project(normalize(track_rows), virt_kv).astype(jnp.bfloat16)
        real_keys = split_heads(key_value[..., :D]).astype(jnp.float32)
        real_values = split_heads(key_value[..., D:]).astype(jnp.float32)
        scores = jnp.einsum('ifhe,bfhe->fihb', virt_query, real_keys) * scaling
        is_visible = (jnp.transpose(seen_now) > 0)[:, None, None, :]
        scores = jnp.where(is_visible, scores, NEG)
        new_peak = jnp.maximum(running_peak, lax.optimization_barrier(jnp.max(scores, -1)))
        exp_terms = jnp.exp(scores - new_peak[..., None]) * is_visible.astype(jnp.float32)
        factor = jnp.exp(running_peak - new_peak)
        denominator = denominator * factor + lax.optimization_barrier(jnp.sum(exp_terms, -1))
        weighted = weighted * factor[..., None] + jnp.einsum('fihb,bfhe->fihe', exp_terms, real_values)
        return ((new_peak, denominator, weighted), None)
    start = (jnp.full((FRAMES, VIRT, HEADS), NEG, jnp.float32), jnp.zeros((FRAMES, VIRT, HEADS), jnp.float32), jnp.zeros((FRAMES, VIRT, HEADS, D // HEADS), jnp.float32))
    (running_peak, denominator, weighted), unused = lax.scan(absorb, start, (updated, seen_blocks))
    attended = (weighted / denominator[..., None]).astype(jnp.bfloat16).reshape(FRAMES, VIRT, D)
    attended = jnp.transpose(attended, (1, 0, 2))
    virt_cross = (virtual.astype(jnp.float32) + project(attended, virt_out)).astype(jnp.bfloat16)
    virtual_out = virtual_self(virt_cross, self_qkv, self_out)
    back_pair = project(normalize(virtual_out), back_kv).astype(jnp.bfloat16)
    back_keys = split_heads(back_pair[..., :D]).astype(jnp.float32)
    back_values = split_heads(back_pair[..., D:]).astype(jnp.float32)

    def finish(track_rows):
        queries = split_heads(project(normalize(track_rows), back_q).astype(jnp.bfloat16)).astype(jnp.float32)
        scores = jnp.einsum('bfhe,ifhe->bfhi', queries, back_keys) * scaling
        weights = jax.nn.softmax(scores, -1).astype(jnp.bfloat16)
        mixed = jnp.einsum('bfhi,ifhe->bfhe', weights.astype(jnp.float32), back_values).astype(jnp.bfloat16)
        mixed = mixed.reshape(track_rows.shape)
        return (track_rows.astype(jnp.float32) + project(mixed, back_out)).astype(jnp.bfloat16)
    tracks_out = lax.map(finish, updated).reshape(number, FRAMES, D)
    return (tracks_out, virtual_out)
```

```python
import jax
import jax.numpy as jnp
from jax import lax
from jax.experimental import pallas as pl
from jax.experimental.pallas import tpu as pltpu
from jax.sharding import Mesh
from jax.sharding import PartitionSpec as P

HEADS = 8
EPS = 1e-05
NEG = -1e30
MARK = 64.0
BF = jnp.bfloat16
F32 = jnp.float32
TRACK_AXES = ("x", "zh", "zl", "c")


def normalize(values):
    widened = values.astype(F32)
    center = jnp.mean(widened, -1, keepdims=True)
    shifted = widened - center
    return (shifted * lax.rsqrt(jnp.mean(shifted * shifted, -1, keepdims=True) + EPS)).astype(BF)


def matmul(a, b):
    return lax.dot_general(a, b, (((1,), (0,)), ((), ())), preferred_element_type=F32)


def matmul_t(a, b):
    return lax.dot_general(a, b, (((1,), (1,)), ((), ())), preferred_element_type=F32)


def iota(shape, dim):
    return lax.broadcasted_iota(jnp.int32, shape, dim)


def head_masks(width):
    lane = iota((1, width), 1)
    each = width // HEADS
    return [(lane >= h * each) & (lane < (h + 1) * each) for h in range(HEADS)]


def stack_heads(rows):
    width = rows.shape[1]
    return jnp.concatenate(
        [rows * mask.astype(F32).astype(rows.dtype) for mask in head_masks(width)], axis=0
    )


def pick_heads(stacked, count):
    masks = head_masks(stacked.shape[1])
    total = jnp.where(masks[0], stacked[:count], 0.0)
    for h in range(1, HEADS):
        total = jnp.where(masks[h], stacked[h * count : (h + 1) * count], total)
    return total


def softmax_mix(scores, values, factor, count):
    peak = jnp.max(scores, -1, keepdims=True)
    terms = jnp.exp((scores - peak) * factor)
    denominator = jnp.sum(terms, -1, keepdims=True)
    mixed = matmul(terms.astype(BF), values)
    return pick_heads(mixed * (1.0 / denominator), count)


def swap_matrix(outer, inner):
    n = outer * inner
    row, col = iota((n, n), 0), iota((n, n), 1)
    source = (row % inner) * outer + row // inner
    return jnp.where(col == source, 1.0, 0.0).astype(BF)


def own_kernel(tokens_ref, virtual_ref, time_qkv_ref, virt_q_ref, qkv_ref, query_ref):
    qkv_ref[...] = matmul(normalize(tokens_ref[...]), time_qkv_ref[...]).astype(BF)
    query_ref[...] = matmul(normalize(virtual_ref[...]), virt_q_ref[...]).astype(BF)


def time_kernel(
    frames, group, tokens_ref, qkv_ref, p1_ref, p2_ref, p3_ref, visible_ref, time_qkv_ref, time_out_ref, back_q_ref,
    updated_ref, send_ref, query_ref,
):
    width = tokens_ref.shape[1]
    factor = float((width // HEADS) ** (-0.5))
    rows = tokens_ref.shape[0]
    tracks = rows // frames
    size = group * frames
    time_kv = time_qkv_ref[:, width:]
    pairs = [qkv_ref[:, width:]] + [
        matmul(normalize(ref[...]), time_kv).astype(BF) for ref in (p1_ref, p2_ref, p3_ref)
    ]
    row, col = iota((size, 4 * size), 0), iota((size, 4 * size), 1)
    bias = jnp.where(row // frames == (col % size) // frames, 0.0, NEG)[None]
    mixed = []
    for g in range(rows // size):
        span = slice(g * size, (g + 1) * size)
        keys = jnp.concatenate([pair[span, :width] for pair in pairs], axis=0)
        values = jnp.concatenate([pair[span, width:] for pair in pairs], axis=0)
        scores = matmul_t(stack_heads(qkv_ref[span, :width]), keys)
        scores = (scores.reshape(HEADS, size, 4 * size) + bias).reshape(HEADS * size, 4 * size)
        mixed.append(softmax_mix(scores, values, factor, size).astype(BF))
    mixed = jnp.concatenate(mixed, axis=0)
    updated = (tokens_ref[...].astype(F32) + matmul(mixed, time_out_ref[...])).astype(BF)
    updated_ref[...] = updated
    by_frame = swap_matrix(frames, tracks)
    normed = matmul(by_frame, normalize(updated))
    pick = jnp.where(iota((rows, tracks), 0) % tracks == iota((rows, tracks), 1), 1.0, 0.0).astype(BF)
    spread = matmul(pick, visible_ref[...].astype(F32).astype(BF))
    here = iota((rows, frames), 0) // tracks == iota((rows, frames), 1)
    seen = jnp.sum(jnp.where(here, spread, 0.0), -1, keepdims=True) > 0.5
    send_ref[...] = jnp.where(seen, normed, MARK).astype(BF)
    query_ref[...] = matmul(normed.astype(BF), back_q_ref[...]).astype(BF)


def partial_kernel(here_ref, there_ref, query_ref, virt_kv_ref, out_ref):
    width = here_ref.shape[1]
    factor = float((width // HEADS) ** (-0.5))
    count = query_ref.shape[0]
    rows = jnp.concatenate([here_ref[...], there_ref[...]], axis=0)
    pair = matmul(rows, virt_kv_ref[...]).astype(BF)
    first = jnp.where(iota((8, width), 1) == 0, 1.0, 0.0).astype(BF)
    seen = matmul_t(first, rows)[:1] < MARK / 2
    scores = matmul_t(stack_heads(query_ref[...]), pair[:, :width])
    scores = jnp.where(seen, scores * factor, NEG)
    peak = jnp.max(scores, -1, keepdims=True)
    terms = jnp.where(seen, jnp.exp(scores - peak), 0.0)
    denominator = jnp.sum(terms, -1, keepdims=True)
    out_ref[:, :width] = pick_heads(matmul(terms.astype(BF), pair[:, width:]), count)
    lane = iota((count, 128), 1)
    stats = jnp.zeros((count, 128), F32)
    for h in range(HEADS):
        span = slice(h * count, (h + 1) * count)
        stats = jnp.where(lane == h, peak[span], stats)
        stats = jnp.where(lane == HEADS + h, denominator[span], stats)
    out_ref[:, width:] = stats


def virtual_kernel(
    a_ref, b_ref, c_ref, d_ref, virtual_ref, virt_out_ref, self_qkv_ref, self_out_ref, out_ref
):
    count, width = virtual_ref.shape
    factor = float((width // HEADS) ** (-0.5))
    parts = [ref[...] for ref in (a_ref, b_ref, c_ref, d_ref)]
    peaks = [part[:, width : width + HEADS] for part in parts]
    sums = [part[:, width + HEADS : width + 2 * HEADS] for part in parts]
    top = jnp.maximum(jnp.maximum(peaks[0], peaks[1]), jnp.maximum(peaks[2], peaks[3]))
    scales = [jnp.exp(peak - top) for peak in peaks]
    denominator = sum(scale * total for scale, total in zip(scales, sums))
    inverse = 1.0 / denominator
    lane = iota((HEADS, width), 1)
    head = iota((HEADS, width), 0)
    each = width // HEADS
    expand = jnp.where((lane >= head * each) & (lane < (head + 1) * each), 1.0, 0.0)
    attended = jnp.zeros((count, width), F32)
    for scale, part in zip(scales, parts):
        weight = lax.dot_general(
            scale * inverse, expand, (((1,), (0,)), ((), ())),
            precision=lax.Precision.HIGHEST, preferred_element_type=F32,
        )
        attended = attended + weight * part[:, :width]
    cross = (virtual_ref[...].astype(F32) + matmul(attended.astype(BF), virt_out_ref[...])).astype(BF)
    proj = matmul(normalize(cross), self_qkv_ref[...]).astype(BF)
    scores = matmul_t(stack_heads(proj[:, :width]), proj[:, width : 2 * width])
    mixed = softmax_mix(scores, proj[:, 2 * width :], factor, count).astype(BF)
    out_ref[...] = (cross.astype(F32) + matmul(mixed, self_out_ref[...])).astype(BF)


def back_kernel(updated_ref, query_ref, virtual_ref, back_kv_ref, back_out_ref, out_ref, virtual_out_ref):
    frames, count, width = virtual_ref.shape
    rows = updated_ref.shape[0]
    tracks = rows // frames
    factor = float((width // HEADS) ** (-0.5))
    flat = virtual_ref[...].reshape(frames * count, width)
    pair = matmul(normalize(flat), back_kv_ref[...]).astype(BF)
    mixed = []
    for f in range(frames):
        span = slice(f * count, (f + 1) * count)
        scores = matmul_t(stack_heads(query_ref[f * tracks : (f + 1) * tracks]), pair[span, :width])
        mixed.append(softmax_mix(scores, pair[span, width:], factor, tracks).astype(BF))
    by_track = matmul(swap_matrix(tracks, frames), jnp.concatenate(mixed, axis=0)).astype(BF)
    out_ref[...] = (updated_ref[...].astype(F32) + matmul(by_track, back_out_ref[...])).astype(BF)
    virtual_out_ref[...] = matmul(swap_matrix(count, frames), flat).astype(BF)


def call(kernel, outs, *args, megabytes=32):
    return pl.pallas_call(
        kernel,
        out_shape=[jax.ShapeDtypeStruct(shape, dtype) for shape, dtype in outs],
        compiler_params=pltpu.CompilerParams(vmem_limit_bytes=megabytes * 1024 * 1024),
    )(*args)


def shift(value, axis, count, step):
    return lax.ppermute(value, axis, [(i, (i + step) % count) for i in range(count)])


def on_device(
    tokens, visible, virtual, time_qkv, time_out, virt_q, virt_kv, virt_out, self_qkv, self_out, back_q, back_kv,
    back_out,
):
    tracks, frames, width = tokens.shape
    count = virtual.shape[0]
    rows = tracks * frames
    flat = tokens.reshape(rows, width)
    others = [shift(flat, "y", 4, step) for step in (1, 3, 2)]
    frame = lax.axis_index("x") * 2 + lax.axis_index("zl")
    mine = lax.dynamic_slice_in_dim(virtual, frame, 1, axis=1).reshape(count, width)
    qkv, virt_query = call(
        own_kernel, [((rows, 3 * width), BF), ((count, width), BF)], flat, mine, time_qkv, virt_q
    )
    updated, send, back_query = call(
        lambda *refs: time_kernel(frames, 8, *refs),
        [((rows, width), BF)] * 3,
        flat, qkv, *others, visible, time_qkv, time_out, back_q,
    )
    got = lax.all_to_all(send.reshape(frames, tracks, width), ("x", "zl"), 0, 0).reshape(rows, width)
    got_there = shift(got, "c", 2, 1)
    (partial,) = call(partial_kernel, [((count, width + 128), F32)], got, got_there, virt_query, virt_kv)
    partials = [partial] + [shift(partial, "zh", 4, step) for step in (1, 3, 2)]
    (frame_out,) = call(
        virtual_kernel, [((count, width), BF)], *partials, mine, virt_out, self_qkv, self_out
    )
    gathered = lax.all_to_all(
        jnp.broadcast_to(frame_out[None], (frames, count, width)), ("x", "zl"), 0, 0
    )
    tracks_out, virtual_out = call(
        back_kernel,
        [((rows, width), BF), ((count * frames, width), BF)],
        updated, back_query, gathered, back_kv, back_out,
    )
    return tracks_out.reshape(tokens.shape), virtual_out.reshape(virtual.shape)


def solution(mesh):
    fine = Mesh(mesh.devices.reshape(4, 4, 2, 2, 4), ("x", "zh", "zl", "c", "y"))
    tokens = P(TRACK_AXES, "y", None)
    virtual = P(None, "y", None)
    return jax.shard_map(
        on_device,
        mesh=fine,
        in_specs=(tokens, P(TRACK_AXES, "y"), virtual) + (P(),) * 10,
        out_specs=(tokens, virtual),
        check_vma=False,
    )
```

```python
import jax
import jax.numpy as jnp
from jax import lax
from jax.experimental import pallas as pl
from jax.experimental.pallas import tpu as pltpu
from jax.sharding import Mesh
from jax.sharding import PartitionSpec as P

HEADS = 8
TILE = 256
EPS = 1e-05
NEG = -1e30
LOG2E = 1.4426950408889634
GROUP = 4
STEPS = (2, 1, 3)
EARLY = 1
ZSTEPS = (1, 3, 2)
MARK = 64.0
BF = jnp.bfloat16
F32 = jnp.float32
TRACK_AXES = ("x", "zh", "zl", "c")


def normalize(values):
    widened = values.astype(F32)
    center = jnp.mean(widened, -1, keepdims=True)
    shifted = widened - center
    return (shifted * lax.rsqrt(jnp.mean(shifted * shifted, -1, keepdims=True) + EPS)).astype(BF)


def matmul(a, b):
    return lax.dot_general(a, b, (((1,), (0,)), ((), ())), preferred_element_type=F32)


def matmul_t(a, b):
    return lax.dot_general(a, b, (((1,), (1,)), ((), ())), preferred_element_type=F32)


def iota(shape, dim):
    return lax.broadcasted_iota(jnp.int32, shape, dim)


def scale_of(width):
    return float((width // HEADS) ** (-0.5)) * LOG2E


def tile(rows, j):
    return rows[:, :TILE] if j == 0 else rows[:, rows.shape[1] - TILE :]


def tile_masks(width, j):
    each = width // HEADS
    lane = iota((1, TILE), 1) + j * (width - TILE)
    return [(lane >= h * each) & (lane < (h + 1) * each) for h in range(4 * j, 4 * j + 4)]


def stack_heads(rows, j):
    part = tile(rows, j)
    return jnp.concatenate(
        [part * mask.astype(F32).astype(rows.dtype) for mask in tile_masks(rows.shape[1], j)], axis=0
    )


def pick_heads(stacked, j, width):
    masks = tile_masks(width, j)
    count = stacked.shape[0] // 4
    total = stacked[:count]
    for k in range(1, 4):
        total = jnp.where(masks[k], stacked[k * count : (k + 1) * count], total)
    return total


def join_tiles(a, b, width):
    middle = jnp.where(iota((1, 128), 1) < width // 2 - 128, a[:, 128:], b[:, :128])
    return jnp.concatenate([a[:, :128], middle, b[:, 128:]], axis=1)


def attend(items, width):
    scale = scale_of(width)
    tiles = [(j, *item) for item in items for j in (0, 1)]
    scores = []
    for j, queries, keys, _, bias in tiles:
        raw = matmul_t(stack_heads(queries, j), tile(keys, j))
        if bias is not None:
            raw = (raw.reshape(4, queries.shape[0], -1) + bias).reshape(raw.shape)
        scores.append(raw)
    terms = [jnp.exp2((raw - jnp.max(raw, -1, keepdims=True)) * scale) for raw in scores]
    mixed = []
    for (j, _, _, values, _), term in zip(tiles, terms):
        share = 1.0 / jnp.sum(term, -1, keepdims=True)
        mixed.append(pick_heads(matmul(term.astype(BF), tile(values, j)) * share, j, width))
    return [join_tiles(a, b, width).astype(BF) for a, b in zip(mixed[::2], mixed[1::2])]


def swap_matrix(outer, inner):
    n = outer * inner
    row, col = iota((n, n), 0), iota((n, n), 1)
    source = (row & (inner - 1)) * outer + (row >> (inner.bit_length() - 1))
    return jnp.where(col == source, 1.0, 0.0).astype(BF)


def own_kernel(tokens_ref, virtual_ref, time_qkv_ref, virt_q_ref, qkv_ref, query_ref):
    qkv_ref[...] = matmul(normalize(tokens_ref[...]), time_qkv_ref[...]).astype(BF)
    query_ref[...] = matmul(normalize(virtual_ref[...]), virt_q_ref[...]).astype(BF)


def pair_kernel(tokens_ref, time_qkv_ref, out_ref):
    width = tokens_ref.shape[1]
    out_ref[...] = matmul(normalize(tokens_ref[...]), time_qkv_ref[:, width:]).astype(BF)


def time_kernel(
    frames, group, early, tokens_ref, qkv_ref, *refs
):
    piece_refs = refs[:3]
    visible_ref, time_qkv_ref, time_out_ref, updated_ref, send_ref, normed_ref = refs[3:]
    rows, width = tokens_ref.shape
    tracks = rows // frames
    size = group * frames
    pairs = [qkv_ref[:, width:]] + [ref[...] for ref in piece_refs[:early]]
    pairs += [matmul(normalize(ref[...]), time_qkv_ref[:, width:]).astype(BF) for ref in piece_refs[early:]]
    row, col = iota((size, 4 * size), 0), iota((size, 4 * size), 1)
    bias = jnp.where(row // frames == (col & (size - 1)) // frames, 0.0, NEG)[None]
    items = []
    for start in range(0, rows, size):
        span = slice(start, start + size)
        keys = jnp.concatenate([pair[span, :width] for pair in pairs], axis=0)
        values = jnp.concatenate([pair[span, width:] for pair in pairs], axis=0)
        items.append((qkv_ref[span, :width], keys, values, bias))
    mixed = jnp.concatenate(attend(items, width), axis=0)
    updated = (tokens_ref[...].astype(F32) + matmul(mixed, time_out_ref[...])).astype(BF)
    updated_ref[...] = updated
    normed = matmul(swap_matrix(frames, tracks), normalize(updated))
    pick = jnp.where((iota((rows, tracks), 0) & (tracks - 1)) == iota((rows, tracks), 1), 1.0, 0.0).astype(BF)
    spread = matmul(pick, visible_ref[...].astype(F32).astype(BF))
    here = iota((rows, frames), 0) // tracks == iota((rows, frames), 1)
    seen = jnp.sum(jnp.where(here, spread, 0.0), -1, keepdims=True) > 0.5
    send_ref[...] = jnp.where(seen, normed, MARK).astype(BF)
    normed_ref[...] = normed.astype(BF)


def split(value):
    high = value.astype(BF)
    rest = value - high.astype(F32)
    middle = rest.astype(BF)
    return [high, middle, (rest - middle.astype(F32)).astype(BF)]


def partial_kernel(here_ref, there_ref, query_ref, virt_kv_ref, out_ref):
    width = here_ref.shape[1]
    count = query_ref.shape[0]
    scale = scale_of(width)
    rows = jnp.concatenate([here_ref[...], there_ref[...]], axis=0)
    pair = matmul(rows, virt_kv_ref[...]).astype(BF)
    first = jnp.where(iota((8, width), 1) == 0, 1.0, 0.0).astype(BF)
    bias = jnp.where(matmul_t(first, rows)[:1] < MARK / 2, 0.0, NEG)
    scores = [matmul_t(stack_heads(query_ref[...], j), tile(pair[:, :width], j)) + bias for j in (0, 1)]
    peaks = [jnp.max(raw, -1, keepdims=True) for raw in scores]
    terms = [jnp.exp2((raw - peak) * scale) for raw, peak in zip(scores, peaks)]
    sums = [jnp.sum(term, -1, keepdims=True) for term in terms]
    mixed = [
        pick_heads(matmul(term.astype(BF), tile(pair[:, width:], j)), j, width) for j, term in enumerate(terms)
    ]
    out_ref[:, :width] = join_tiles(*mixed, width).astype(BF)
    lane = iota((count, 128), 1)
    peak, total = jnp.zeros((count, 128), F32), jnp.zeros((count, 128), F32)
    for h in range(HEADS):
        span = slice(h % 4 * count, (h % 4 + 1) * count)
        peak = jnp.where((lane & 7) == h, peaks[h // 4][span], peak)
        total = jnp.where((lane & 7) == h, sums[h // 4][span], total)
    stats = jnp.zeros((count, 128), F32)
    for k, piece in enumerate(split(peak) + split(total)):
        stats = jnp.where(lane >> 3 == k, piece.astype(F32), stats)
    out_ref[:, width:] = stats.astype(BF)


def merge(parts, width):
    scale = scale_of(width)
    each = width // HEADS
    lane, column = iota((128, width), 0), iota((128, width), 1)
    mine = (column >= (lane & 7) * each) & (column < ((lane & 7) + 1) * each)
    spread_peak = jnp.where(mine & (lane < 24), 1.0, 0.0).astype(BF)
    spread_sum = jnp.where(mine & (lane >= 24) & (lane < 48), 1.0, 0.0).astype(BF)
    peaks = [matmul(part[:, width:], spread_peak) for part in parts]
    sums = [matmul(part[:, width:], spread_sum) for part in parts]
    top = peaks[0]
    for peak in peaks[1:]:
        top = jnp.maximum(top, peak)
    weighted, denominator = 0.0, 0.0
    for part, peak, total in zip(parts, peaks, sums):
        weight = jnp.exp2((peak - top) * scale)
        weighted = weighted + weight * part[:, :width].astype(F32)
        denominator = denominator + weight * total
    return (weighted / denominator).astype(BF)


def virtual_kernel(*refs):
    *part_refs, virtual_ref, virt_out_ref, self_qkv_ref, self_out_ref, out_ref = refs
    width = virtual_ref.shape[1]
    attended = merge([ref[...] for ref in part_refs], width)
    cross = (virtual_ref[...].astype(F32) + matmul(attended, virt_out_ref[...])).astype(BF)
    proj = matmul(normalize(cross), self_qkv_ref[...]).astype(BF)
    (mixed,) = attend([(proj[:, :width], proj[:, width : 2 * width], proj[:, 2 * width :], None)], width)
    out_ref[...] = (cross.astype(F32) + matmul(mixed, self_out_ref[...])).astype(BF)


def back_kernel(
    updated_ref, normed_ref, virtual_ref, back_q_ref, back_kv_ref, back_out_ref, out_ref, virtual_out_ref
):
    frames, count, width = virtual_ref.shape
    rows = updated_ref.shape[0]
    tracks = rows // frames
    query = matmul(normed_ref[...], back_q_ref[...]).astype(BF)
    flat = virtual_ref[...].reshape(frames * count, width)
    pair = matmul(normalize(flat), back_kv_ref[...]).astype(BF)
    items = []
    for f in range(frames):
        span = slice(f * count, (f + 1) * count)
        items.append((query[f * tracks : (f + 1) * tracks], pair[span, :width], pair[span, width:], None))
    mixed = jnp.concatenate(attend(items, width), axis=0)
    by_track = matmul(swap_matrix(tracks, frames), mixed).astype(BF)
    out_ref[...] = (updated_ref[...].astype(F32) + matmul(by_track, back_out_ref[...])).astype(BF)
    step = count // 4
    for start in range(0, count, step):
        block = jnp.concatenate([virtual_ref[f, start : start + step] for f in range(frames)], axis=0)
        virtual_out_ref[start * frames : (start + step) * frames] = matmul(
            swap_matrix(step, frames), block
        ).astype(BF)


def call(kernel, outs, *args, megabytes=32):
    return pl.pallas_call(
        kernel,
        out_shape=[jax.ShapeDtypeStruct(shape, dtype) for shape, dtype in outs],
        compiler_params=pltpu.CompilerParams(vmem_limit_bytes=megabytes * 1024 * 1024),
    )(*args)


def shift(value, axis, count, step):
    return lax.ppermute(value, axis, [(i, (i + step) % count) for i in range(count)])


def on_device(
    tokens, visible, virtual, time_qkv, time_out, virt_q, virt_kv, virt_out, self_qkv, self_out, back_q, back_kv,
    back_out,
):
    tracks, frames, width = tokens.shape
    count = virtual.shape[0]
    rows = tracks * frames
    flat = tokens.reshape(rows, width)
    others = [shift(flat, "y", 4, step) for step in STEPS]
    frame = lax.axis_index("x") * 2 + lax.axis_index("zl")
    mine = lax.dynamic_slice_in_dim(virtual, frame, 1, axis=1).reshape(count, width)
    qkv, virt_query = call(
        own_kernel, [((rows, 3 * width), BF), ((count, width), BF)], flat, mine, time_qkv, virt_q
    )
    for k in range(EARLY):
        (others[k],) = call(pair_kernel, [((rows, 2 * width), BF)], others[k], time_qkv)
    updated, send, normed = call(
        lambda *refs: time_kernel(frames, GROUP, EARLY, *refs),
        [((rows, width), BF)] * 3,
        flat, qkv, *others, visible, time_qkv, time_out,
    )
    got = lax.all_to_all(send.reshape(frames, tracks, width), ("x", "zl"), 0, 0).reshape(rows, width)
    got_there = shift(got, "c", 2, 1)
    (partial,) = call(partial_kernel, [((count, width + 128), BF)], got, got_there, virt_query, virt_kv)
    partials = [partial] + [shift(partial, "zh", 4, step) for step in ZSTEPS]
    (frame_out,) = call(
        virtual_kernel, [((count, width), BF)], *partials, mine, virt_out, self_qkv, self_out
    )
    gathered = lax.all_to_all(
        jnp.broadcast_to(frame_out[None], (frames, count, width)), ("x", "zl"), 0, 0
    )
    tracks_out, virtual_out = call(
        back_kernel,
        [((rows, width), BF), ((count * frames, width), BF)],
        updated, normed, gathered, back_q, back_kv, back_out,
    )
    return tracks_out.reshape(tokens.shape), virtual_out.reshape(virtual.shape)


def solution(mesh):
    fine = Mesh(mesh.devices.reshape(4, 4, 2, 2, 4), ("x", "zh", "zl", "c", "y"))
    tokens = P(TRACK_AXES, "y", None)
    virtual = P(None, "y", None)
    return jax.shard_map(
        on_device,
        mesh=fine,
        in_specs=(tokens, P(TRACK_AXES, "y"), virtual) + (P(),) * 10,
        out_specs=(tokens, virtual),
        check_vma=False,
    )
```

```python
import jax
import jax.numpy as jnp
from jax import lax
from jax.experimental import pallas as pl
from jax.experimental.pallas import tpu as pltpu
from jax.sharding import Mesh
from jax.sharding import PartitionSpec as P

HEADS = 8
TILE = 256
EPS = 1e-05
NEG = -1e30
LOG2E = 1.4426950408889634
GROUP = 4
STEPS = (2, 1, 3)
EARLY = 1
ZSTEPS = (1, 3, 2)
MARK = 64.0
BF = jnp.bfloat16
F32 = jnp.float32
TRACK_AXES = ("x", "zh", "zl", "c")


def normalize(values):
    widened = values.astype(F32)
    center = jnp.mean(widened, -1, keepdims=True)
    shifted = widened - center
    return (shifted * lax.rsqrt(jnp.mean(shifted * shifted, -1, keepdims=True) + EPS)).astype(BF)


def matmul(a, b):
    return lax.dot_general(a, b, (((1,), (0,)), ((), ())), preferred_element_type=F32)


def matmul_t(a, b):
    return lax.dot_general(a, b, (((1,), (1,)), ((), ())), preferred_element_type=F32)


def iota(shape, dim):
    return lax.broadcasted_iota(jnp.int32, shape, dim)


def scale_of(width):
    return float((width // HEADS) ** (-0.5)) * LOG2E


def tile(rows, j):
    return rows[:, :TILE] if j == 0 else rows[:, rows.shape[1] - TILE :]


def tile_masks(width, j):
    each = width // HEADS
    lane = iota((1, TILE), 1) + j * (width - TILE)
    return [(lane >= h * each) & (lane < (h + 1) * each) for h in range(4 * j, 4 * j + 4)]


def stack_heads(rows, j):
    part = tile(rows, j)
    return jnp.concatenate(
        [part * mask.astype(F32).astype(rows.dtype) for mask in tile_masks(rows.shape[1], j)], axis=0
    )


def pick_heads(stacked, j, width):
    masks = tile_masks(width, j)
    count = stacked.shape[0] // 4
    total = stacked[:count]
    for k in range(1, 4):
        total = jnp.where(masks[k], stacked[k * count : (k + 1) * count], total)
    return total


def join_tiles(a, b, width):
    middle = jnp.where(iota((1, 128), 1) < width // 2 - 128, a[:, 128:], b[:, :128])
    return jnp.concatenate([a[:, :128], middle, b[:, 128:]], axis=1)


def attend(items, width):
    scale = scale_of(width)
    tiles = [(j, *item) for item in items for j in (0, 1)]
    scores = []
    for j, queries, keys, _, bias in tiles:
        raw = matmul_t(stack_heads(queries, j), tile(keys, j))
        if bias is not None:
            raw = (raw.reshape(4, queries.shape[0], -1) + bias).reshape(raw.shape)
        scores.append(raw)
    terms = [jnp.exp2((raw - jnp.max(raw, -1, keepdims=True)) * scale) for raw in scores]
    mixed = []
    for (j, _, _, values, _), term in zip(tiles, terms):
        share = 1.0 / jnp.sum(term, -1, keepdims=True)
        mixed.append(pick_heads(matmul(term.astype(BF), tile(values, j)) * share, j, width))
    return [join_tiles(a, b, width).astype(BF) for a, b in zip(mixed[::2], mixed[1::2])]


def swap_matrix(outer, inner):
    n = outer * inner
    row, col = iota((n, n), 0), iota((n, n), 1)
    source = (row & (inner - 1)) * outer + (row >> (inner.bit_length() - 1))
    return jnp.where(col == source, 1.0, 0.0).astype(BF)


def own_kernel(tokens_ref, virtual_ref, time_qkv_ref, virt_q_ref, qkv_ref, query_ref):
    qkv_ref[...] = matmul(normalize(tokens_ref[...]), time_qkv_ref[...]).astype(BF)
    query_ref[...] = matmul(normalize(virtual_ref[...]), virt_q_ref[...]).astype(BF)


def pair_kernel(tokens_ref, time_qkv_ref, out_ref):
    width = tokens_ref.shape[1]
    out_ref[...] = matmul(normalize(tokens_ref[...]), time_qkv_ref[:, width:]).astype(BF)


def time_kernel(
    frames, group, early, tokens_ref, qkv_ref, *refs
):
    piece_refs = refs[:3]
    visible_ref, time_qkv_ref, time_out_ref, updated_ref, send_ref, normed_ref = refs[3:]
    rows, width = tokens_ref.shape
    tracks = rows // frames
    size = group * frames
    pairs = [qkv_ref[:, width:]] + [ref[...] for ref in piece_refs[:early]]
    pairs += [matmul(normalize(ref[...]), time_qkv_ref[:, width:]).astype(BF) for ref in piece_refs[early:]]
    row, col = iota((size, 4 * size), 0), iota((size, 4 * size), 1)
    bias = jnp.where(row // frames == (col & (size - 1)) // frames, 0.0, NEG)[None]
    items = []
    for start in range(0, rows, size):
        span = slice(start, start + size)
        keys = jnp.concatenate([pair[span, :width] for pair in pairs], axis=0)
        values = jnp.concatenate([pair[span, width:] for pair in pairs], axis=0)
        items.append((qkv_ref[span, :width], keys, values, bias))
    mixed = jnp.concatenate(attend(items, width), axis=0)
    updated = (tokens_ref[...].astype(F32) + matmul(mixed, time_out_ref[...])).astype(BF)
    updated_ref[...] = updated
    normed = matmul(swap_matrix(frames, tracks), normalize(updated))
    pick = jnp.where((iota((rows, tracks), 0) & (tracks - 1)) == iota((rows, tracks), 1), 1.0, 0.0).astype(BF)
    spread = matmul(pick, visible_ref[...].astype(F32).astype(BF))
    here = iota((rows, frames), 0) // tracks == iota((rows, frames), 1)
    seen = jnp.sum(jnp.where(here, spread, 0.0), -1, keepdims=True) > 0.5
    send_ref[...] = jnp.where(seen, normed, MARK).astype(BF)
    normed_ref[...] = normed.astype(BF)


def split(value):
    high = value.astype(BF)
    rest = value - high.astype(F32)
    middle = rest.astype(BF)
    return [high, middle, (rest - middle.astype(F32)).astype(BF)]


def pack_stats(peak, total):
    lane = iota(peak.shape, 1)
    stats = jnp.zeros(peak.shape, F32)
    for k, piece in enumerate(split(peak) + split(total)):
        stats = jnp.where(lane >> 3 == k, piece.astype(F32), stats)
    return stats.astype(BF)


def partial_kernel(rows_ref, query_ref, virt_kv_ref, out_ref):
    rows = rows_ref[...]
    width = rows.shape[1]
    count = query_ref.shape[0]
    scale = scale_of(width)
    pair = matmul(rows, virt_kv_ref[...]).astype(BF)
    first = jnp.where(iota((8, width), 1) == 0, 1.0, 0.0).astype(BF)
    bias = jnp.where(matmul_t(first, rows)[:1] < MARK / 2, 0.0, NEG)
    scores = [matmul_t(stack_heads(query_ref[...], j), tile(pair[:, :width], j)) + bias for j in (0, 1)]
    peaks = [jnp.max(raw, -1, keepdims=True) for raw in scores]
    terms = [jnp.exp2((raw - peak) * scale) for raw, peak in zip(scores, peaks)]
    sums = [jnp.sum(term, -1, keepdims=True) for term in terms]
    mixed = [
        pick_heads(matmul(term.astype(BF), tile(pair[:, width:], j)), j, width) for j, term in enumerate(terms)
    ]
    out_ref[:, :width] = join_tiles(*mixed, width).astype(BF)
    lane = iota((count, 128), 1)
    peak, total = jnp.zeros((count, 128), F32), jnp.zeros((count, 128), F32)
    for h in range(HEADS):
        span = slice(h % 4 * count, (h % 4 + 1) * count)
        peak = jnp.where((lane & 7) == h, peaks[h // 4][span], peak)
        total = jnp.where((lane & 7) == h, sums[h // 4][span], total)
    out_ref[:, width:] = pack_stats(peak, total)


def merge(parts, width):
    scale = scale_of(width)
    each = width // HEADS
    lane, column = iota((128, width), 0), iota((128, width), 1)
    mine = (column >= (lane & 7) * each) & (column < ((lane & 7) + 1) * each)
    spread_peak = jnp.where(mine & (lane < 24), 1.0, 0.0).astype(BF)
    spread_sum = jnp.where(mine & (lane >= 24) & (lane < 48), 1.0, 0.0).astype(BF)
    peaks = [matmul(part[:, width:], spread_peak) for part in parts]
    sums = [matmul(part[:, width:], spread_sum) for part in parts]
    top = peaks[0]
    for peak in peaks[1:]:
        top = jnp.maximum(top, peak)
    weighted, denominator = 0.0, 0.0
    for part, peak, total in zip(parts, peaks, sums):
        weight = jnp.exp2((peak - top) * scale)
        weighted = weighted + weight * part[:, :width].astype(F32)
        denominator = denominator + weight * total
    return (weighted / denominator).astype(BF)


def both_kernel(a_ref, b_ref, out_ref):
    width = a_ref.shape[1] - 128
    scale = scale_of(width)
    each = width // HEADS
    source, lane = iota((128, 256), 0), iota((128, 256), 1)
    same = (source & 7) == (lane & 7)
    here = ((lane < 128) & (source < 24)) | ((lane >= 128) & (source >= 24) & (source < 48))
    gather = jnp.where(same & here, 1.0, 0.0).astype(BF)
    parts = [a_ref[...], b_ref[...]]
    stats = [matmul(part[:, width:], gather) for part in parts]
    peaks, sums = [s[:, :128] for s in stats], [s[:, 128:] for s in stats]
    top = jnp.maximum(*peaks)
    weights = [jnp.exp2((peak - top) * scale) for peak in peaks]
    lane, column = iota((128, width), 0), iota((128, width), 1)
    spread = jnp.where(
        (column >= (lane & 7) * each) & (column < ((lane & 7) + 1) * each) & (lane < 16), 1.0, 0.0
    ).astype(BF)
    total, mixed = 0.0, 0.0
    for part, weight, count in zip(parts, weights, sums):
        high = weight.astype(BF)
        low = weight - high.astype(F32)
        pieces = jnp.where(iota(weight.shape, 1) < 8, high.astype(F32), low).astype(BF)
        mixed = mixed + matmul(pieces, spread) * part[:, :width].astype(F32)
        total = total + weight * count
    out_ref[:, :width] = mixed.astype(BF)
    out_ref[:, width:] = pack_stats(top, total)


def virtual_kernel(*refs):
    _, *part_refs, virtual_ref, virt_out_ref, self_qkv_ref, self_out_ref, out_ref = refs
    width = virtual_ref.shape[1]
    attended = merge([ref[...] for ref in part_refs], width)
    cross = (virtual_ref[...].astype(F32) + matmul(attended, virt_out_ref[...])).astype(BF)
    proj = matmul(normalize(cross), self_qkv_ref[...]).astype(BF)
    (mixed,) = attend([(proj[:, :width], proj[:, width : 2 * width], proj[:, 2 * width :], None)], width)
    out_ref[...] = (cross.astype(F32) + matmul(mixed, self_out_ref[...])).astype(BF)


def query_kernel(normed_ref, back_q_ref, out_ref):
    out_ref[...] = matmul(normed_ref[...], back_q_ref[...]).astype(BF)


def back_kernel(
    updated_ref, query_ref, virtual_ref, back_kv_ref, back_out_ref, out_ref, virtual_out_ref
):
    frames, count, width = virtual_ref.shape
    rows = updated_ref.shape[0]
    tracks = rows // frames
    step = count // 4
    for start in range(0, count, step):
        block = jnp.concatenate([virtual_ref[f, start : start + step] for f in range(frames)], axis=0)
        virtual_out_ref[start * frames : (start + step) * frames] = matmul(
            swap_matrix(step, frames), block
        ).astype(BF)
    query = query_ref[...]
    flat = virtual_ref[...].reshape(frames * count, width)
    pair = matmul(normalize(flat), back_kv_ref[...]).astype(BF)
    items = []
    for f in range(frames):
        span = slice(f * count, (f + 1) * count)
        items.append((query[f * tracks : (f + 1) * tracks], pair[span, :width], pair[span, width:], None))
    mixed = jnp.concatenate(attend(items, width), axis=0)
    by_track = matmul(swap_matrix(tracks, frames), mixed).astype(BF)
    out_ref[...] = (updated_ref[...].astype(F32) + matmul(by_track, back_out_ref[...])).astype(BF)


def call(kernel, outs, *args, megabytes=32):
    return pl.pallas_call(
        kernel,
        out_shape=[jax.ShapeDtypeStruct(shape, dtype) for shape, dtype in outs],
        compiler_params=pltpu.CompilerParams(vmem_limit_bytes=megabytes * 1024 * 1024),
    )(*args)


def shift(value, axis, count, step):
    return lax.ppermute(value, axis, [(i, (i + step) % count) for i in range(count)])


def on_device(
    tokens, visible, virtual, time_qkv, time_out, virt_q, virt_kv, virt_out, self_qkv, self_out, back_q, back_kv,
    back_out,
):
    tracks, frames, width = tokens.shape
    count = virtual.shape[0]
    rows = tracks * frames
    flat = tokens.reshape(rows, width)
    others = [shift(flat, "y", 4, step) for step in STEPS]
    frame = lax.axis_index("x") * 2 + lax.axis_index("zl")
    mine = lax.dynamic_slice_in_dim(virtual, frame, 1, axis=1).reshape(count, width)
    qkv, virt_query = call(
        own_kernel, [((rows, 3 * width), BF), ((count, width), BF)], flat, mine, time_qkv, virt_q
    )
    for k in range(EARLY):
        (others[k],) = call(pair_kernel, [((rows, 2 * width), BF)], others[k], time_qkv)
    updated, send, normed = call(
        lambda *refs: time_kernel(frames, GROUP, EARLY, *refs),
        [((rows, width), BF)] * 3,
        flat, qkv, *others, visible, time_qkv, time_out,
    )
    got = lax.all_to_all(send.reshape(frames, tracks, width), ("x", "zl"), 0, 0).reshape(rows, width)
    (partial,) = call(partial_kernel, [((count, width + 128), BF)], got, virt_query, virt_kv)
    (partial,) = call(both_kernel, [((count, width + 128), BF)], partial, shift(partial, "c", 2, 1))
    (query,) = call(query_kernel, [((rows, width), BF)], normed, back_q)
    partials = [partial] + [lax.ppermute(partial, "zh", [(i, i ^ k) for i in range(4)]) for k in ZSTEPS]
    (frame_out,) = call(
        virtual_kernel, [((count, width), BF)], query, *partials, mine, virt_out, self_qkv, self_out
    )
    gathered = lax.all_to_all(
        jnp.broadcast_to(frame_out[None], (frames, count, width)), ("x", "zl"), 0, 0
    )
    tracks_out, virtual_out = call(
        back_kernel,
        [((rows, width), BF), ((count * frames, width), BF)],
        updated, query, gathered, back_kv, back_out,
    )
    return tracks_out.reshape(tokens.shape), virtual_out.reshape(virtual.shape)


def solution(mesh):
    fine = Mesh(mesh.devices.reshape(4, 4, 2, 2, 4), ("x", "zh", "zl", "c", "y"))
    tokens = P(TRACK_AXES, "y", None)
    virtual = P(None, "y", None)
    return jax.shard_map(
        on_device,
        mesh=fine,
        in_specs=(tokens, P(TRACK_AXES, "y"), virtual) + (P(),) * 10,
        out_specs=(tokens, virtual),
        check_vma=False,
    )
```

```python
import jax
import jax.numpy as jnp
from jax import lax
from jax.experimental import pallas as pl
from jax.experimental.pallas import tpu as pltpu
from jax.sharding import Mesh
from jax.sharding import PartitionSpec as P

HEADS = 8
TILE = 256
EPS = 1e-05
NEG = -1e30
LOG2E = 1.4426950408889634
GROUP = 4
STEPS = (2, 1, 3)
EARLY = 1
MARK = 64.0
BF = jnp.bfloat16
F32 = jnp.float32
TRACK_AXES = ("x", "zh", "zl", "c")


def normalize(values):
    widened = values.astype(F32)
    center = jnp.mean(widened, -1, keepdims=True)
    shifted = widened - center
    return (shifted * lax.rsqrt(jnp.mean(shifted * shifted, -1, keepdims=True) + EPS)).astype(BF)


def matmul(a, b):
    return lax.dot_general(a, b, (((1,), (0,)), ((), ())), preferred_element_type=F32)


def matmul_t(a, b):
    return lax.dot_general(a, b, (((1,), (1,)), ((), ())), preferred_element_type=F32)


def iota(shape, dim):
    return lax.broadcasted_iota(jnp.int32, shape, dim)


def scale_of(width):
    return float((width // HEADS) ** (-0.5)) * LOG2E


def tile(rows, j):
    return rows[:, :TILE] if j == 0 else rows[:, rows.shape[1] - TILE :]


def tile_masks(width, j):
    each = width // HEADS
    lane = iota((1, TILE), 1) + j * (width - TILE)
    return [(lane >= h * each) & (lane < (h + 1) * each) for h in range(4 * j, 4 * j + 4)]


def stack_heads(rows, j):
    part = tile(rows, j)
    return jnp.concatenate(
        [part * mask.astype(F32).astype(rows.dtype) for mask in tile_masks(rows.shape[1], j)], axis=0
    )


def pick_heads(stacked, j, width):
    masks = tile_masks(width, j)
    count = stacked.shape[0] // 4
    total = stacked[:count]
    for k in range(1, 4):
        total = jnp.where(masks[k], stacked[k * count : (k + 1) * count], total)
    return total


def join_tiles(a, b, width):
    middle = jnp.where(iota((1, 128), 1) < width // 2 - 128, a[:, 128:], b[:, :128])
    return jnp.concatenate([a[:, :128], middle, b[:, 128:]], axis=1)


def attend(items, width):
    scale = scale_of(width)
    tiles = [(j, *item) for item in items for j in (0, 1)]
    scores = []
    for j, queries, keys, _, bias in tiles:
        raw = matmul_t(stack_heads(queries, j), tile(keys, j))
        if bias is not None:
            raw = (raw.reshape(4, queries.shape[0], -1) + bias).reshape(raw.shape)
        scores.append(raw)
    terms = [jnp.exp2((raw - jnp.max(raw, -1, keepdims=True)) * scale) for raw in scores]
    mixed = []
    for (j, _, _, values, _), term in zip(tiles, terms):
        share = 1.0 / jnp.sum(term, -1, keepdims=True)
        mixed.append(pick_heads(matmul(term.astype(BF), tile(values, j)) * share, j, width))
    return [join_tiles(a, b, width).astype(BF) for a, b in zip(mixed[::2], mixed[1::2])]


def swap_matrix(outer, inner):
    n = outer * inner
    row, col = iota((n, n), 0), iota((n, n), 1)
    source = (row & (inner - 1)) * outer + (row >> (inner.bit_length() - 1))
    return jnp.where(col == source, 1.0, 0.0).astype(BF)


def own_kernel(tokens_ref, virtual_ref, time_qkv_ref, virt_q_ref, qkv_ref, query_ref):
    qkv_ref[...] = matmul(normalize(tokens_ref[...]), time_qkv_ref[...]).astype(BF)
    query_ref[...] = matmul(normalize(virtual_ref[...]), virt_q_ref[...]).astype(BF)


def pair_kernel(tokens_ref, time_qkv_ref, out_ref):
    width = tokens_ref.shape[1]
    out_ref[...] = matmul(normalize(tokens_ref[...]), time_qkv_ref[:, width:]).astype(BF)


def time_kernel(
    frames, group, early, tokens_ref, qkv_ref, *refs
):
    piece_refs = refs[:3]
    visible_ref, time_qkv_ref, time_out_ref, updated_ref, send_ref, normed_ref = refs[3:]
    rows, width = tokens_ref.shape
    tracks = rows // frames
    size = group * frames
    pairs = [qkv_ref[:, width:]] + [ref[...] for ref in piece_refs[:early]]
    pairs += [matmul(normalize(ref[...]), time_qkv_ref[:, width:]).astype(BF) for ref in piece_refs[early:]]
    row, col = iota((size, 4 * size), 0), iota((size, 4 * size), 1)
    bias = jnp.where(row // frames == (col & (size - 1)) // frames, 0.0, NEG)[None]
    items = []
    for start in range(0, rows, size):
        span = slice(start, start + size)
        keys = jnp.concatenate([pair[span, :width] for pair in pairs], axis=0)
        values = jnp.concatenate([pair[span, width:] for pair in pairs], axis=0)
        items.append((qkv_ref[span, :width], keys, values, bias))
    mixed = jnp.concatenate(attend(items, width), axis=0)
    updated = (tokens_ref[...].astype(F32) + matmul(mixed, time_out_ref[...])).astype(BF)
    updated_ref[...] = updated
    normed = matmul(swap_matrix(frames, tracks), normalize(updated))
    pick = jnp.where((iota((rows, tracks), 0) & (tracks - 1)) == iota((rows, tracks), 1), 1.0, 0.0).astype(BF)
    spread = matmul(pick, visible_ref[...].astype(F32).astype(BF))
    here = iota((rows, frames), 0) // tracks == iota((rows, frames), 1)
    seen = jnp.sum(jnp.where(here, spread, 0.0), -1, keepdims=True) > 0.5
    send_ref[...] = jnp.where(seen, normed, MARK).astype(BF)
    normed_ref[...] = normed.astype(BF)


def split(value):
    high = value.astype(BF)
    rest = value - high.astype(F32)
    middle = rest.astype(BF)
    return [high, middle, (rest - middle.astype(F32)).astype(BF)]


def pack_stats(peak, total):
    lane = iota(peak.shape, 1)
    stats = jnp.zeros(peak.shape, F32)
    for k, piece in enumerate(split(peak) + split(total)):
        stats = jnp.where(lane >> 3 == k, piece.astype(F32), stats)
    return stats.astype(BF)


def partial_kernel(rows_ref, query_ref, virt_kv_ref, out_ref):
    rows = rows_ref[...]
    width = rows.shape[1]
    count = query_ref.shape[0]
    scale = scale_of(width)
    pair = matmul(rows, virt_kv_ref[...]).astype(BF)
    first = jnp.where(iota((8, width), 1) == 0, 1.0, 0.0).astype(BF)
    bias = jnp.where(matmul_t(first, rows)[:1] < MARK / 2, 0.0, NEG)
    scores = [matmul_t(stack_heads(query_ref[...], j), tile(pair[:, :width], j)) + bias for j in (0, 1)]
    peaks = [jnp.max(raw, -1, keepdims=True) for raw in scores]
    terms = [jnp.exp2((raw - peak) * scale) for raw, peak in zip(scores, peaks)]
    sums = [jnp.sum(term, -1, keepdims=True) for term in terms]
    mixed = [
        pick_heads(matmul(term.astype(BF), tile(pair[:, width:], j)), j, width) for j, term in enumerate(terms)
    ]
    out_ref[:, :width] = join_tiles(*mixed, width).astype(BF)
    lane = iota((count, 128), 1)
    peak, total = jnp.zeros((count, 128), F32), jnp.zeros((count, 128), F32)
    for h in range(HEADS):
        span = slice(h % 4 * count, (h % 4 + 1) * count)
        peak = jnp.where((lane & 7) == h, peaks[h // 4][span], peak)
        total = jnp.where((lane & 7) == h, sums[h // 4][span], total)
    out_ref[:, width:] = pack_stats(peak, total)


def merge(parts, width):
    scale = scale_of(width)
    each = width // HEADS
    lane, column = iota((128, width), 0), iota((128, width), 1)
    mine = (column >= (lane & 7) * each) & (column < ((lane & 7) + 1) * each)
    spread_peak = jnp.where(mine & (lane < 24), 1.0, 0.0).astype(BF)
    spread_sum = jnp.where(mine & (lane >= 24) & (lane < 48), 1.0, 0.0).astype(BF)
    peaks = [matmul(part[:, width:], spread_peak) for part in parts]
    sums = [matmul(part[:, width:], spread_sum) for part in parts]
    top = peaks[0]
    for peak in peaks[1:]:
        top = jnp.maximum(top, peak)
    weighted, denominator = 0.0, 0.0
    for part, peak, total in zip(parts, peaks, sums):
        weight = jnp.exp2((peak - top) * scale)
        weighted = weighted + weight * part[:, :width].astype(F32)
        denominator = denominator + weight * total
    return (weighted / denominator).astype(BF)


def both_kernel(a_ref, b_ref, out_ref):
    width = a_ref.shape[1] - 128
    scale = scale_of(width)
    each = width // HEADS
    source, lane = iota((128, 256), 0), iota((128, 256), 1)
    same = (source & 7) == (lane & 7)
    here = ((lane < 128) & (source < 24)) | ((lane >= 128) & (source >= 24) & (source < 48))
    gather = jnp.where(same & here, 1.0, 0.0).astype(BF)
    parts = [a_ref[...], b_ref[...]]
    stats = [matmul(part[:, width:], gather) for part in parts]
    peaks, sums = [s[:, :128] for s in stats], [s[:, 128:] for s in stats]
    top = jnp.maximum(*peaks)
    weights = [jnp.exp2((peak - top) * scale) for peak in peaks]
    lane, column = iota((128, width), 0), iota((128, width), 1)
    spread = jnp.where(
        (column >= (lane & 7) * each) & (column < ((lane & 7) + 1) * each) & (lane < 16), 1.0, 0.0
    ).astype(BF)
    total, mixed = 0.0, 0.0
    for part, weight, count in zip(parts, weights, sums):
        high = weight.astype(BF)
        low = weight - high.astype(F32)
        pieces = jnp.where(iota(weight.shape, 1) < 8, high.astype(F32), low).astype(BF)
        mixed = mixed + matmul(pieces, spread) * part[:, :width].astype(F32)
        total = total + weight * count
    out_ref[:, :width] = mixed.astype(BF)
    out_ref[:, width:] = pack_stats(top, total)


def virtual_kernel(*refs):
    _, *part_refs, virtual_ref, virt_out_ref, self_qkv_ref, self_out_ref, out_ref = refs
    width = virtual_ref.shape[1]
    attended = merge([ref[...] for ref in part_refs], width)
    cross = (virtual_ref[...].astype(F32) + matmul(attended, virt_out_ref[...])).astype(BF)
    proj = matmul(normalize(cross), self_qkv_ref[...]).astype(BF)
    (mixed,) = attend([(proj[:, :width], proj[:, width : 2 * width], proj[:, 2 * width :], None)], width)
    out_ref[...] = (cross.astype(F32) + matmul(mixed, self_out_ref[...])).astype(BF)


def query_kernel(normed_ref, back_q_ref, out_ref):
    out_ref[...] = matmul(normed_ref[...], back_q_ref[...]).astype(BF)


def back_kernel(
    updated_ref, query_ref, virtual_ref, back_kv_ref, back_out_ref, out_ref, virtual_out_ref
):
    frames, count, width = virtual_ref.shape
    rows = updated_ref.shape[0]
    tracks = rows // frames
    step = count // 4
    for start in range(0, count, step):
        block = jnp.concatenate([virtual_ref[f, start : start + step] for f in range(frames)], axis=0)
        virtual_out_ref[start * frames : (start + step) * frames] = matmul(
            swap_matrix(step, frames), block
        ).astype(BF)
    query = query_ref[...]
    flat = virtual_ref[...].reshape(frames * count, width)
    pair = matmul(normalize(flat), back_kv_ref[...]).astype(BF)
    items = []
    for f in range(frames):
        span = slice(f * count, (f + 1) * count)
        items.append((query[f * tracks : (f + 1) * tracks], pair[span, :width], pair[span, width:], None))
    mixed = jnp.concatenate(attend(items, width), axis=0)
    by_track = matmul(swap_matrix(tracks, frames), mixed).astype(BF)
    out_ref[...] = (updated_ref[...].astype(F32) + matmul(by_track, back_out_ref[...])).astype(BF)


def call(kernel, outs, *args, megabytes=32):
    return pl.pallas_call(
        kernel,
        out_shape=[jax.ShapeDtypeStruct(shape, dtype) for shape, dtype in outs],
        compiler_params=pltpu.CompilerParams(vmem_limit_bytes=megabytes * 1024 * 1024),
    )(*args)


def shift(value, axis, count, step):
    return lax.ppermute(value, axis, [(i, (i + step) % count) for i in range(count)])


def on_device(
    tokens, visible, virtual, time_qkv, time_out, virt_q, virt_kv, virt_out, self_qkv, self_out, back_q, back_kv,
    back_out,
):
    tracks, frames, width = tokens.shape
    count = virtual.shape[0]
    rows = tracks * frames
    flat = tokens.reshape(rows, width)
    others = [shift(flat, "y", 4, step) for step in STEPS]
    frame = lax.axis_index("x") * 2 + lax.axis_index("zl")
    mine = lax.dynamic_slice_in_dim(virtual, frame, 1, axis=1).reshape(count, width)
    qkv, virt_query = call(
        own_kernel, [((rows, 3 * width), BF), ((count, width), BF)], flat, mine, time_qkv, virt_q
    )
    for k in range(EARLY):
        (others[k],) = call(pair_kernel, [((rows, 2 * width), BF)], others[k], time_qkv)
    updated, send, normed = call(
        lambda *refs: time_kernel(frames, GROUP, EARLY, *refs),
        [((rows, width), BF)] * 3,
        flat, qkv, *others, visible, time_qkv, time_out,
    )
    got = lax.all_to_all(send.reshape(frames, tracks, width), ("x", "zl"), 0, 0).reshape(rows, width)
    (partial,) = call(partial_kernel, [((count, width + 128), BF)], got, virt_query, virt_kv)
    (partial,) = call(both_kernel, [((count, width + 128), BF)], partial, shift(partial, "c", 2, 1))
    (query,) = call(query_kernel, [((rows, width), BF)], normed, back_q)
    split_pairs = [(z * 2 + c, (z ^ (2, 3)[c]) * 2 + c) for z in range(4) for c in range(2)]
    fetched = lax.ppermute(partial, ("zh", "c"), split_pairs)
    near = lax.ppermute(partial, "zh", [(z, z ^ 1) for z in range(4)])
    partials = [partial, fetched, shift(fetched, "c", 2, 1), near]
    (frame_out,) = call(
        virtual_kernel, [((count, width), BF)], query, *partials, mine, virt_out, self_qkv, self_out
    )
    gathered = lax.all_to_all(
        jnp.broadcast_to(frame_out[None], (frames, count, width)), ("x", "zl"), 0, 0
    )
    tracks_out, virtual_out = call(
        back_kernel,
        [((rows, width), BF), ((count * frames, width), BF)],
        updated, query, gathered, back_kv, back_out,
    )
    return tracks_out.reshape(tokens.shape), virtual_out.reshape(virtual.shape)


def solution(mesh):
    fine = Mesh(mesh.devices.reshape(4, 4, 2, 2, 4), ("x", "zh", "zl", "c", "y"))
    tokens = P(TRACK_AXES, "y", None)
    virtual = P(None, "y", None)
    return jax.shard_map(
        on_device,
        mesh=fine,
        in_specs=(tokens, P(TRACK_AXES, "y"), virtual) + (P(),) * 10,
        out_specs=(tokens, virtual),
        check_vma=False,
    )
```

```python
import jax
import jax.numpy as jnp
from jax import lax
from jax.experimental import pallas as pl
from jax.experimental.pallas import tpu as pltpu
from jax.sharding import Mesh
from jax.sharding import PartitionSpec as P

HEADS = 8
TILE = 256
EPS = 1e-05
NEG = -1e30
LOG2E = 1.4426950408889634
GROUP = 4
STEPS = (2, 1, 3)
EARLY = 1
GATHER_STEPS = (4, 2, 6)
MARK = 64.0
BF = jnp.bfloat16
F32 = jnp.float32
TRACK_AXES = ("x", "zh", "zl", "c")


def normalize(values):
    widened = values.astype(F32)
    center = jnp.mean(widened, -1, keepdims=True)
    shifted = widened - center
    return (shifted * lax.rsqrt(jnp.mean(shifted * shifted, -1, keepdims=True) + EPS)).astype(BF)


def matmul(a, b):
    return lax.dot_general(a, b, (((1,), (0,)), ((), ())), preferred_element_type=F32)


def matmul_t(a, b):
    return lax.dot_general(a, b, (((1,), (1,)), ((), ())), preferred_element_type=F32)


def iota(shape, dim):
    return lax.broadcasted_iota(jnp.int32, shape, dim)


def scale_of(width):
    return float((width // HEADS) ** (-0.5)) * LOG2E


def tile(rows, j):
    return rows[:, :TILE] if j == 0 else rows[:, rows.shape[1] - TILE :]


def tile_masks(width, j):
    each = width // HEADS
    lane = iota((1, TILE), 1) + j * (width - TILE)
    return [(lane >= h * each) & (lane < (h + 1) * each) for h in range(4 * j, 4 * j + 4)]


def stack_heads(rows, j):
    part = tile(rows, j)
    return jnp.concatenate(
        [part * mask.astype(F32).astype(rows.dtype) for mask in tile_masks(rows.shape[1], j)], axis=0
    )


def pick_heads(stacked, j, width):
    masks = tile_masks(width, j)
    count = stacked.shape[0] // 4
    total = stacked[:count]
    for k in range(1, 4):
        total = jnp.where(masks[k], stacked[k * count : (k + 1) * count], total)
    return total


def join_tiles(a, b, width):
    middle = jnp.where(iota((1, 128), 1) < width // 2 - 128, a[:, 128:], b[:, :128])
    return jnp.concatenate([a[:, :128], middle, b[:, 128:]], axis=1)


def attend(items, width):
    scale = scale_of(width)
    tiles = [(j, *item) for item in items for j in (0, 1)]
    scores = []
    for j, queries, keys, _, bias in tiles:
        raw = matmul_t(stack_heads(queries, j), tile(keys, j))
        if bias is not None:
            raw = (raw.reshape(4, queries.shape[0], -1) + bias).reshape(raw.shape)
        scores.append(raw)
    terms = [jnp.exp2((raw - jnp.max(raw, -1, keepdims=True)) * scale) for raw in scores]
    mixed = []
    for (j, _, _, values, _), term in zip(tiles, terms):
        share = 1.0 / jnp.sum(term, -1, keepdims=True)
        mixed.append(pick_heads(matmul(term.astype(BF), tile(values, j)) * share, j, width))
    return [join_tiles(a, b, width).astype(BF) for a, b in zip(mixed[::2], mixed[1::2])]


def swap_matrix(outer, inner):
    n = outer * inner
    row, col = iota((n, n), 0), iota((n, n), 1)
    source = (row & (inner - 1)) * outer + (row >> (inner.bit_length() - 1))
    return jnp.where(col == source, 1.0, 0.0).astype(BF)


def own_kernel(tokens_ref, virtual_ref, time_qkv_ref, virt_q_ref, qkv_ref, query_ref):
    qkv_ref[...] = matmul(normalize(tokens_ref[...]), time_qkv_ref[...]).astype(BF)
    query_ref[...] = matmul(normalize(virtual_ref[...]), virt_q_ref[...]).astype(BF)


def pair_kernel(tokens_ref, time_qkv_ref, out_ref):
    width = tokens_ref.shape[1]
    out_ref[...] = matmul(normalize(tokens_ref[...]), time_qkv_ref[:, width:]).astype(BF)


def time_kernel(
    frames, group, early, tokens_ref, qkv_ref, *refs
):
    piece_refs = refs[:3]
    visible_ref, time_qkv_ref, time_out_ref, updated_ref, send_ref, normed_ref = refs[3:]
    rows, width = tokens_ref.shape
    tracks = rows // frames
    size = group * frames
    pairs = [qkv_ref[:, width:]] + [ref[...] for ref in piece_refs[:early]]
    pairs += [matmul(normalize(ref[...]), time_qkv_ref[:, width:]).astype(BF) for ref in piece_refs[early:]]
    row, col = iota((size, 4 * size), 0), iota((size, 4 * size), 1)
    bias = jnp.where(row // frames == (col & (size - 1)) // frames, 0.0, NEG)[None]
    items = []
    for start in range(0, rows, size):
        span = slice(start, start + size)
        keys = jnp.concatenate([pair[span, :width] for pair in pairs], axis=0)
        values = jnp.concatenate([pair[span, width:] for pair in pairs], axis=0)
        items.append((qkv_ref[span, :width], keys, values, bias))
    mixed = jnp.concatenate(attend(items, width), axis=0)
    updated = (tokens_ref[...].astype(F32) + matmul(mixed, time_out_ref[...])).astype(BF)
    updated_ref[...] = updated
    normed = matmul(swap_matrix(frames, tracks), normalize(updated))
    pick = jnp.where((iota((rows, tracks), 0) & (tracks - 1)) == iota((rows, tracks), 1), 1.0, 0.0).astype(BF)
    spread = matmul(pick, visible_ref[...].astype(F32).astype(BF))
    here = iota((rows, frames), 0) // tracks == iota((rows, frames), 1)
    seen = jnp.sum(jnp.where(here, spread, 0.0), -1, keepdims=True) > 0.5
    send_ref[...] = jnp.where(seen, normed, MARK).astype(BF)
    normed_ref[...] = normed.astype(BF)


def split(value):
    high = value.astype(BF)
    rest = value - high.astype(F32)
    middle = rest.astype(BF)
    return [high, middle, (rest - middle.astype(F32)).astype(BF)]


def pack_stats(peak, total):
    lane = iota(peak.shape, 1)
    stats = jnp.zeros(peak.shape, F32)
    for k, piece in enumerate(split(peak) + split(total)):
        stats = jnp.where(lane >> 3 == k, piece.astype(F32), stats)
    return stats.astype(BF)


def partial_kernel(rows_ref, query_ref, virt_kv_ref, out_ref):
    rows = rows_ref[...]
    width = rows.shape[1]
    count = query_ref.shape[0]
    scale = scale_of(width)
    pair = matmul(rows, virt_kv_ref[...]).astype(BF)
    first = jnp.where(iota((8, width), 1) == 0, 1.0, 0.0).astype(BF)
    bias = jnp.where(matmul_t(first, rows)[:1] < MARK / 2, 0.0, NEG)
    scores = [matmul_t(stack_heads(query_ref[...], j), tile(pair[:, :width], j)) + bias for j in (0, 1)]
    peaks = [jnp.max(raw, -1, keepdims=True) for raw in scores]
    terms = [jnp.exp2((raw - peak) * scale) for raw, peak in zip(scores, peaks)]
    sums = [jnp.sum(term, -1, keepdims=True) for term in terms]
    mixed = [
        pick_heads(matmul(term.astype(BF), tile(pair[:, width:], j)), j, width) for j, term in enumerate(terms)
    ]
    out_ref[:, :width] = join_tiles(*mixed, width).astype(BF)
    lane = iota((count, 128), 1)
    peak, total = jnp.zeros((count, 128), F32), jnp.zeros((count, 128), F32)
    for h in range(HEADS):
        span = slice(h % 4 * count, (h % 4 + 1) * count)
        peak = jnp.where((lane & 7) == h, peaks[h // 4][span], peak)
        total = jnp.where((lane & 7) == h, sums[h // 4][span], total)
    out_ref[:, width:] = pack_stats(peak, total)


def merge(parts, width):
    scale = scale_of(width)
    each = width // HEADS
    lane, column = iota((128, width), 0), iota((128, width), 1)
    mine = (column >= (lane & 7) * each) & (column < ((lane & 7) + 1) * each)
    spread_peak = jnp.where(mine & (lane < 24), 1.0, 0.0).astype(BF)
    spread_sum = jnp.where(mine & (lane >= 24) & (lane < 48), 1.0, 0.0).astype(BF)
    peaks = [matmul(part[:, width:], spread_peak) for part in parts]
    sums = [matmul(part[:, width:], spread_sum) for part in parts]
    top = peaks[0]
    for peak in peaks[1:]:
        top = jnp.maximum(top, peak)
    weighted, denominator = 0.0, 0.0
    for part, peak, total in zip(parts, peaks, sums):
        weight = jnp.exp2((peak - top) * scale)
        weighted = weighted + weight * part[:, :width].astype(F32)
        denominator = denominator + weight * total
    return (weighted / denominator).astype(BF)


def both_kernel(a_ref, b_ref, out_ref):
    width = a_ref.shape[1] - 128
    scale = scale_of(width)
    each = width // HEADS
    source, lane = iota((128, 256), 0), iota((128, 256), 1)
    same = (source & 7) == (lane & 7)
    here = ((lane < 128) & (source < 24)) | ((lane >= 128) & (source >= 24) & (source < 48))
    gather = jnp.where(same & here, 1.0, 0.0).astype(BF)
    parts = [a_ref[...], b_ref[...]]
    stats = [matmul(part[:, width:], gather) for part in parts]
    peaks, sums = [s[:, :128] for s in stats], [s[:, 128:] for s in stats]
    top = jnp.maximum(*peaks)
    weights = [jnp.exp2((peak - top) * scale) for peak in peaks]
    lane, column = iota((128, width), 0), iota((128, width), 1)
    spread = jnp.where(
        (column >= (lane & 7) * each) & (column < ((lane & 7) + 1) * each) & (lane < 16), 1.0, 0.0
    ).astype(BF)
    total, mixed = 0.0, 0.0
    for part, weight, count in zip(parts, weights, sums):
        high = weight.astype(BF)
        low = weight - high.astype(F32)
        pieces = jnp.where(iota(weight.shape, 1) < 8, high.astype(F32), low).astype(BF)
        mixed = mixed + matmul(pieces, spread) * part[:, :width].astype(F32)
        total = total + weight * count
    out_ref[:, :width] = mixed.astype(BF)
    out_ref[:, width:] = pack_stats(top, total)


def virtual_kernel(*refs):
    _, *part_refs, virtual_ref, virt_out_ref, self_qkv_ref, self_out_ref, out_ref = refs
    width = virtual_ref.shape[1]
    attended = merge([ref[...] for ref in part_refs], width)
    cross = (virtual_ref[...].astype(F32) + matmul(attended, virt_out_ref[...])).astype(BF)
    proj = matmul(normalize(cross), self_qkv_ref[...]).astype(BF)
    (mixed,) = attend([(proj[:, :width], proj[:, width : 2 * width], proj[:, 2 * width :], None)], width)
    out_ref[...] = (cross.astype(F32) + matmul(mixed, self_out_ref[...])).astype(BF)


def query_kernel(place_ref, normed_ref, back_q_ref, out_ref, swap_part_ref, swap_ref):
    frame, core = place_ref[0], place_ref[1]
    rows = normed_ref.shape[0]
    frames = 8
    tracks = rows // frames

    def turn(place):
        return jnp.where(place >= 2, place ^ core, place)

    def swap(n):
        row, col = iota((n, n), 0), iota((n, n), 1)
        source = turn((row & (frames - 1)) ^ frame) * (n // frames) + (row >> (frames.bit_length() - 1))
        return jnp.where(col == source, 1.0, 0.0).astype(BF)

    swap_part_ref[...] = swap(swap_part_ref.shape[0])
    swap_ref[...] = swap(rows)
    starts = [pl.multiple_of((turn(jnp.int32(place)) ^ frame) * tracks, tracks) for place in range(frames)]
    ordered = jnp.concatenate([normed_ref[pl.ds(start, tracks)] for start in starts], axis=0)
    out_ref[...] = matmul(ordered, back_q_ref[...]).astype(BF)


def back_kernel(updated_ref, query_ref, swap_part_ref, swap_ref, *refs):
    *piece_refs, back_kv_ref, back_out_ref, out_ref, virtual_out_ref = refs
    frames = len(piece_refs)
    count, width = piece_refs[0].shape
    tracks = updated_ref.shape[0] // frames
    step = swap_part_ref.shape[0] // frames
    for start in range(0, count, step):
        block = jnp.concatenate([ref[start : start + step] for ref in piece_refs], axis=0)
        virtual_out_ref[start * frames : (start + step) * frames] = matmul(swap_part_ref[...], block).astype(BF)
    flat = jnp.concatenate([ref[...] for ref in piece_refs], axis=0)
    pair = matmul(normalize(flat), back_kv_ref[...]).astype(BF)
    items = []
    for place in range(frames):
        span = slice(place * count, (place + 1) * count)
        queries = query_ref[place * tracks : (place + 1) * tracks]
        items.append((queries, pair[span, :width], pair[span, width:], None))
    mixed = jnp.concatenate(attend(items, width), axis=0)
    by_track = matmul(swap_ref[...], mixed).astype(BF)
    out_ref[...] = (updated_ref[...].astype(F32) + matmul(by_track, back_out_ref[...])).astype(BF)


def call(kernel, outs, *args, megabytes=32):
    spaces = [pltpu.SMEM if arg.dtype == jnp.int32 and arg.ndim == 1 else pltpu.VMEM for arg in args]
    return pl.pallas_call(
        kernel,
        out_shape=[jax.ShapeDtypeStruct(shape, dtype) for shape, dtype in outs],
        in_specs=[pl.BlockSpec(memory_space=space) for space in spaces],
        compiler_params=pltpu.CompilerParams(vmem_limit_bytes=megabytes * 1024 * 1024),
    )(*args)


def shift(value, axis, count, step):
    return lax.ppermute(value, axis, [(i, (i + step) % count) for i in range(count)])


def on_device(
    tokens, visible, virtual, time_qkv, time_out, virt_q, virt_kv, virt_out, self_qkv, self_out, back_q, back_kv,
    back_out,
):
    tracks, frames, width = tokens.shape
    count = virtual.shape[0]
    rows = tracks * frames
    flat = tokens.reshape(rows, width)
    others = [shift(flat, "y", 4, step) for step in STEPS]
    frame = lax.axis_index("x") * 2 + lax.axis_index("zl")
    mine = lax.dynamic_slice_in_dim(virtual, frame, 1, axis=1).reshape(count, width)
    qkv, virt_query = call(
        own_kernel, [((rows, 3 * width), BF), ((count, width), BF)], flat, mine, time_qkv, virt_q
    )
    for k in range(EARLY):
        (others[k],) = call(pair_kernel, [((rows, 2 * width), BF)], others[k], time_qkv)
    updated, send, normed = call(
        lambda *refs: time_kernel(frames, GROUP, EARLY, *refs),
        [((rows, width), BF)] * 3,
        flat, qkv, *others, visible, time_qkv, time_out,
    )
    got = lax.all_to_all(send.reshape(frames, tracks, width), ("x", "zl"), 0, 0).reshape(rows, width)
    (partial,) = call(partial_kernel, [((count, width + 128), BF)], got, virt_query, virt_kv)
    (partial,) = call(both_kernel, [((count, width + 128), BF)], partial, shift(partial, "c", 2, 1))
    place = jnp.stack([frame, lax.axis_index("c")]).astype(jnp.int32)
    query, swap_part, swap = call(
        query_kernel, [((rows, width), BF), ((2 * count, 2 * count), BF), ((rows, rows), BF)], place, normed, back_q
    )
    split_pairs = [(z * 2 + c, (z ^ (2, 3)[c]) * 2 + c) for z in range(4) for c in range(2)]
    fetched = lax.ppermute(partial, ("zh", "c"), split_pairs)
    near = lax.ppermute(partial, "zh", [(z, z ^ 1) for z in range(4)])
    partials = [partial, fetched, shift(fetched, "c", 2, 1), near]
    (frame_out,) = call(
        virtual_kernel, [((count, width), BF)], query, *partials, mine, virt_out, self_qkv, self_out
    )
    pieces = [frame_out] + [None] * (frames - 1)
    for k in GATHER_STEPS:
        pairs = [(f * 2 + c, (f ^ (k + c)) * 2 + c) for f in range(frames) for c in range(2)]
        pieces[k] = lax.ppermute(frame_out, ("x", "zl", "c"), pairs)
    pieces[1] = lax.ppermute(frame_out, "zl", [(0, 1), (1, 0)])
    for k in GATHER_STEPS:
        pieces[k + 1] = shift(pieces[k], "c", 2, 1)
    tracks_out, virtual_out = call(
        back_kernel,
        [((rows, width), BF), ((count * frames, width), BF)],
        updated, query, swap_part, swap, *pieces, back_kv, back_out,
    )
    return tracks_out.reshape(tokens.shape), virtual_out.reshape(virtual.shape)


def solution(mesh):
    fine = Mesh(mesh.devices.reshape(4, 4, 2, 2, 4), ("x", "zh", "zl", "c", "y"))
    tokens = P(TRACK_AXES, "y", None)
    virtual = P(None, "y", None)
    return jax.shard_map(
        on_device,
        mesh=fine,
        in_specs=(tokens, P(TRACK_AXES, "y"), virtual) + (P(),) * 10,
        out_specs=(tokens, virtual),
        check_vma=False,
    )
```

```python
import jax
import jax.numpy as jnp
from jax import lax
from jax.experimental import pallas as pl
from jax.experimental.pallas import tpu as pltpu
from jax.sharding import Mesh
from jax.sharding import PartitionSpec as P

HEADS = 8
TILE = 256
EPS = 1e-05
NEG = -1e30
LOG2E = 1.4426950408889634
GROUP = 4
STEPS = (2, 1, 3)
EARLY = 1
GATHER_STEPS = (4, 2, 6)
FIRST_PLACES = (0, 1, 6, 7)
MARK = 64.0
BF = jnp.bfloat16
F32 = jnp.float32
TRACK_AXES = ("x", "zh", "zl", "c")


def normalize(values):
    widened = values.astype(F32)
    center = jnp.mean(widened, -1, keepdims=True)
    shifted = widened - center
    return (shifted * lax.rsqrt(jnp.mean(shifted * shifted, -1, keepdims=True) + EPS)).astype(BF)


def matmul(a, b):
    return lax.dot_general(a, b, (((1,), (0,)), ((), ())), preferred_element_type=F32)


def matmul_t(a, b):
    return lax.dot_general(a, b, (((1,), (1,)), ((), ())), preferred_element_type=F32)


def iota(shape, dim):
    return lax.broadcasted_iota(jnp.int32, shape, dim)


def scale_of(width):
    return float((width // HEADS) ** (-0.5)) * LOG2E


def tile(rows, j):
    return rows[:, :TILE] if j == 0 else rows[:, rows.shape[1] - TILE :]


def tile_masks(width, j):
    each = width // HEADS
    lane = iota((1, TILE), 1) + j * (width - TILE)
    return [(lane >= h * each) & (lane < (h + 1) * each) for h in range(4 * j, 4 * j + 4)]


def stack_heads(rows, j):
    part = tile(rows, j)
    return jnp.concatenate(
        [part * mask.astype(F32).astype(rows.dtype) for mask in tile_masks(rows.shape[1], j)], axis=0
    )


def pick_heads(stacked, j, width):
    masks = tile_masks(width, j)
    count = stacked.shape[0] // 4
    total = stacked[:count]
    for k in range(1, 4):
        total = jnp.where(masks[k], stacked[k * count : (k + 1) * count], total)
    return total


def join_tiles(a, b, width):
    middle = jnp.where(iota((1, 128), 1) < width // 2 - 128, a[:, 128:], b[:, :128])
    return jnp.concatenate([a[:, :128], middle, b[:, 128:]], axis=1)


def attend(items, width):
    scale = scale_of(width)
    tiles = [(j, *item) for item in items for j in (0, 1)]
    scores = []
    for j, queries, keys, _, bias in tiles:
        raw = matmul_t(stack_heads(queries, j), tile(keys, j))
        if bias is not None:
            raw = (raw.reshape(4, queries.shape[0], -1) + bias).reshape(raw.shape)
        scores.append(raw)
    terms = [jnp.exp2((raw - jnp.max(raw, -1, keepdims=True)) * scale) for raw in scores]
    mixed = []
    for (j, _, _, values, _), term in zip(tiles, terms):
        share = 1.0 / jnp.sum(term, -1, keepdims=True)
        mixed.append(pick_heads(matmul(term.astype(BF), tile(values, j)) * share, j, width))
    return [join_tiles(a, b, width).astype(BF) for a, b in zip(mixed[::2], mixed[1::2])]


def swap_matrix(outer, inner):
    n = outer * inner
    row, col = iota((n, n), 0), iota((n, n), 1)
    source = (row & (inner - 1)) * outer + (row >> (inner.bit_length() - 1))
    return jnp.where(col == source, 1.0, 0.0).astype(BF)


def own_kernel(tokens_ref, virtual_ref, time_qkv_ref, virt_q_ref, qkv_ref, query_ref):
    qkv_ref[...] = matmul(normalize(tokens_ref[...]), time_qkv_ref[...]).astype(BF)
    query_ref[...] = matmul(normalize(virtual_ref[...]), virt_q_ref[...]).astype(BF)


def pair_kernel(tokens_ref, time_qkv_ref, out_ref):
    width = tokens_ref.shape[1]
    out_ref[...] = matmul(normalize(tokens_ref[...]), time_qkv_ref[:, width:]).astype(BF)


def time_kernel(
    frames, group, early, tokens_ref, qkv_ref, *refs
):
    piece_refs = refs[:3]
    visible_ref, time_qkv_ref, time_out_ref, updated_ref, send_ref, normed_ref = refs[3:]
    rows, width = tokens_ref.shape
    tracks = rows // frames
    size = group * frames
    pairs = [qkv_ref[:, width:]] + [ref[...] for ref in piece_refs[:early]]
    pairs += [matmul(normalize(ref[...]), time_qkv_ref[:, width:]).astype(BF) for ref in piece_refs[early:]]
    row, col = iota((size, 4 * size), 0), iota((size, 4 * size), 1)
    bias = jnp.where(row // frames == (col & (size - 1)) // frames, 0.0, NEG)[None]
    items = []
    for start in range(0, rows, size):
        span = slice(start, start + size)
        keys = jnp.concatenate([pair[span, :width] for pair in pairs], axis=0)
        values = jnp.concatenate([pair[span, width:] for pair in pairs], axis=0)
        items.append((qkv_ref[span, :width], keys, values, bias))
    mixed = jnp.concatenate(attend(items, width), axis=0)
    updated = (tokens_ref[...].astype(F32) + matmul(mixed, time_out_ref[...])).astype(BF)
    updated_ref[...] = updated
    normed = matmul(swap_matrix(frames, tracks), normalize(updated))
    pick = jnp.where((iota((rows, tracks), 0) & (tracks - 1)) == iota((rows, tracks), 1), 1.0, 0.0).astype(BF)
    spread = matmul(pick, visible_ref[...].astype(F32).astype(BF))
    here = iota((rows, frames), 0) // tracks == iota((rows, frames), 1)
    seen = jnp.sum(jnp.where(here, spread, 0.0), -1, keepdims=True) > 0.5
    send_ref[...] = jnp.where(seen, normed, MARK).astype(BF)
    normed_ref[...] = normed.astype(BF)


def split(value):
    high = value.astype(BF)
    rest = value - high.astype(F32)
    middle = rest.astype(BF)
    return [high, middle, (rest - middle.astype(F32)).astype(BF)]


def pack_stats(peak, total):
    lane = iota(peak.shape, 1)
    stats = jnp.zeros(peak.shape, F32)
    for k, piece in enumerate(split(peak) + split(total)):
        stats = jnp.where(lane >> 3 == k, piece.astype(F32), stats)
    return stats.astype(BF)


def partial_kernel(rows_ref, query_ref, virt_kv_ref, out_ref):
    rows = rows_ref[...]
    width = rows.shape[1]
    count = query_ref.shape[0]
    scale = scale_of(width)
    pair = matmul(rows, virt_kv_ref[...]).astype(BF)
    first = jnp.where(iota((8, width), 1) == 0, 1.0, 0.0).astype(BF)
    bias = jnp.where(matmul_t(first, rows)[:1] < MARK / 2, 0.0, NEG)
    scores = [matmul_t(stack_heads(query_ref[...], j), tile(pair[:, :width], j)) + bias for j in (0, 1)]
    peaks = [jnp.max(raw, -1, keepdims=True) for raw in scores]
    terms = [jnp.exp2((raw - peak) * scale) for raw, peak in zip(scores, peaks)]
    sums = [jnp.sum(term, -1, keepdims=True) for term in terms]
    mixed = [
        pick_heads(matmul(term.astype(BF), tile(pair[:, width:], j)), j, width) for j, term in enumerate(terms)
    ]
    out_ref[:, :width] = join_tiles(*mixed, width).astype(BF)
    lane = iota((count, 128), 1)
    peak, total = jnp.zeros((count, 128), F32), jnp.zeros((count, 128), F32)
    for h in range(HEADS):
        span = slice(h % 4 * count, (h % 4 + 1) * count)
        peak = jnp.where((lane & 7) == h, peaks[h // 4][span], peak)
        total = jnp.where((lane & 7) == h, sums[h // 4][span], total)
    out_ref[:, width:] = pack_stats(peak, total)


def merge(parts, width):
    scale = scale_of(width)
    each = width // HEADS
    lane, column = iota((128, width), 0), iota((128, width), 1)
    mine = (column >= (lane & 7) * each) & (column < ((lane & 7) + 1) * each)
    spread_peak = jnp.where(mine & (lane < 24), 1.0, 0.0).astype(BF)
    spread_sum = jnp.where(mine & (lane >= 24) & (lane < 48), 1.0, 0.0).astype(BF)
    peaks = [matmul(part[:, width:], spread_peak) for part in parts]
    sums = [matmul(part[:, width:], spread_sum) for part in parts]
    top = peaks[0]
    for peak in peaks[1:]:
        top = jnp.maximum(top, peak)
    weighted, denominator = 0.0, 0.0
    for part, peak, total in zip(parts, peaks, sums):
        weight = jnp.exp2((peak - top) * scale)
        weighted = weighted + weight * part[:, :width].astype(F32)
        denominator = denominator + weight * total
    return (weighted / denominator).astype(BF)


def both_kernel(a_ref, b_ref, out_ref):
    width = a_ref.shape[1] - 128
    scale = scale_of(width)
    each = width // HEADS
    source, lane = iota((128, 256), 0), iota((128, 256), 1)
    same = (source & 7) == (lane & 7)
    here = ((lane < 128) & (source < 24)) | ((lane >= 128) & (source >= 24) & (source < 48))
    gather = jnp.where(same & here, 1.0, 0.0).astype(BF)
    parts = [a_ref[...], b_ref[...]]
    stats = [matmul(part[:, width:], gather) for part in parts]
    peaks, sums = [s[:, :128] for s in stats], [s[:, 128:] for s in stats]
    top = jnp.maximum(*peaks)
    weights = [jnp.exp2((peak - top) * scale) for peak in peaks]
    lane, column = iota((128, width), 0), iota((128, width), 1)
    spread = jnp.where(
        (column >= (lane & 7) * each) & (column < ((lane & 7) + 1) * each) & (lane < 16), 1.0, 0.0
    ).astype(BF)
    total, mixed = 0.0, 0.0
    for part, weight, count in zip(parts, weights, sums):
        high = weight.astype(BF)
        low = weight - high.astype(F32)
        pieces = jnp.where(iota(weight.shape, 1) < 8, high.astype(F32), low).astype(BF)
        mixed = mixed + matmul(pieces, spread) * part[:, :width].astype(F32)
        total = total + weight * count
    out_ref[:, :width] = mixed.astype(BF)
    out_ref[:, width:] = pack_stats(top, total)


def virtual_kernel(*refs):
    _, *part_refs, virtual_ref, virt_out_ref, self_qkv_ref, self_out_ref, out_ref = refs
    width = virtual_ref.shape[1]
    attended = merge([ref[...] for ref in part_refs], width)
    cross = (virtual_ref[...].astype(F32) + matmul(attended, virt_out_ref[...])).astype(BF)
    proj = matmul(normalize(cross), self_qkv_ref[...]).astype(BF)
    (mixed,) = attend([(proj[:, :width], proj[:, width : 2 * width], proj[:, 2 * width :], None)], width)
    out_ref[...] = (cross.astype(F32) + matmul(mixed, self_out_ref[...])).astype(BF)


def query_kernel(place_ref, normed_ref, back_q_ref, out_ref, swap_part_ref, swap_ref):
    frame, core = place_ref[0], place_ref[1]
    rows = normed_ref.shape[0]
    frames = 8
    tracks = rows // frames

    def turn(place):
        return jnp.where(place >= 2, place ^ core, place)

    def swap(n):
        row, col = iota((n, n), 0), iota((n, n), 1)
        source = turn((row & (frames - 1)) ^ frame) * (n // frames) + (row >> (frames.bit_length() - 1))
        return jnp.where(col == source, 1.0, 0.0).astype(BF)

    swap_part_ref[...] = swap(swap_part_ref.shape[0])
    swap_ref[...] = swap(rows)
    starts = [pl.multiple_of((turn(jnp.int32(place)) ^ frame) * tracks, tracks) for place in range(frames)]
    ordered = jnp.concatenate([normed_ref[pl.ds(start, tracks)] for start in starts], axis=0)
    out_ref[...] = matmul(ordered, back_q_ref[...]).astype(BF)


def attend_pieces(places, tracks, query_ref, piece_refs, back_kv_ref):
    count, width = piece_refs[0].shape
    flat = jnp.concatenate([ref[...] for ref in piece_refs], axis=0)
    pair = matmul(normalize(flat), back_kv_ref[...]).astype(BF)
    items = []
    for k, place in enumerate(places):
        span = slice(k * count, (k + 1) * count)
        queries = query_ref[place * tracks : (place + 1) * tracks]
        items.append((queries, pair[span, :width], pair[span, width:], None))
    return attend(items, width)


def front_kernel(query_ref, *refs):
    *piece_refs, back_kv_ref, out_ref = refs
    tracks = out_ref.shape[0] // len(FIRST_PLACES)
    out_ref[...] = jnp.concatenate(
        attend_pieces(FIRST_PLACES, tracks, query_ref, piece_refs, back_kv_ref), axis=0
    )


def back_kernel(updated_ref, query_ref, swap_part_ref, swap_ref, front_ref, *refs):
    *piece_refs, back_kv_ref, back_out_ref, out_ref, virtual_out_ref = refs
    frames = len(piece_refs)
    count = piece_refs[0].shape[0]
    tracks = updated_ref.shape[0] // frames
    step = swap_part_ref.shape[0] // frames
    for start in range(0, count, step):
        block = jnp.concatenate([ref[start : start + step] for ref in piece_refs], axis=0)
        virtual_out_ref[start * frames : (start + step) * frames] = matmul(swap_part_ref[...], block).astype(BF)
    rest = [place for place in range(frames) if place not in FIRST_PLACES]
    mixed = dict(zip(rest, attend_pieces(rest, tracks, query_ref, [piece_refs[k] for k in rest], back_kv_ref)))
    for k, place in enumerate(FIRST_PLACES):
        mixed[place] = front_ref[k * tracks : (k + 1) * tracks]
    mixed = jnp.concatenate([mixed[place] for place in range(frames)], axis=0)
    by_track = matmul(swap_ref[...], mixed).astype(BF)
    out_ref[...] = (updated_ref[...].astype(F32) + matmul(by_track, back_out_ref[...])).astype(BF)


def call(kernel, outs, *args, megabytes=32):
    spaces = [pltpu.SMEM if arg.dtype == jnp.int32 and arg.ndim == 1 else pltpu.VMEM for arg in args]
    return pl.pallas_call(
        kernel,
        out_shape=[jax.ShapeDtypeStruct(shape, dtype) for shape, dtype in outs],
        in_specs=[pl.BlockSpec(memory_space=space) for space in spaces],
        compiler_params=pltpu.CompilerParams(vmem_limit_bytes=megabytes * 1024 * 1024),
    )(*args)


def shift(value, axis, count, step):
    return lax.ppermute(value, axis, [(i, (i + step) % count) for i in range(count)])


def on_device(
    tokens, visible, virtual, time_qkv, time_out, virt_q, virt_kv, virt_out, self_qkv, self_out, back_q, back_kv,
    back_out,
):
    tracks, frames, width = tokens.shape
    count = virtual.shape[0]
    rows = tracks * frames
    flat = tokens.reshape(rows, width)
    others = [shift(flat, "y", 4, step) for step in STEPS]
    frame = lax.axis_index("x") * 2 + lax.axis_index("zl")
    mine = lax.dynamic_slice_in_dim(virtual, frame, 1, axis=1).reshape(count, width)
    qkv, virt_query = call(
        own_kernel, [((rows, 3 * width), BF), ((count, width), BF)], flat, mine, time_qkv, virt_q
    )
    for k in range(EARLY):
        (others[k],) = call(pair_kernel, [((rows, 2 * width), BF)], others[k], time_qkv)
    updated, send, normed = call(
        lambda *refs: time_kernel(frames, GROUP, EARLY, *refs),
        [((rows, width), BF)] * 3,
        flat, qkv, *others, visible, time_qkv, time_out,
    )
    got = lax.all_to_all(send.reshape(frames, tracks, width), ("x", "zl"), 0, 0).reshape(rows, width)
    (partial,) = call(partial_kernel, [((count, width + 128), BF)], got, virt_query, virt_kv)
    (partial,) = call(both_kernel, [((count, width + 128), BF)], partial, shift(partial, "c", 2, 1))
    place = jnp.stack([frame, lax.axis_index("c")]).astype(jnp.int32)
    query, swap_part, swap = call(
        query_kernel, [((rows, width), BF), ((2 * count, 2 * count), BF), ((rows, rows), BF)], place, normed, back_q
    )
    split_pairs = [(z * 2 + c, (z ^ (2, 3)[c]) * 2 + c) for z in range(4) for c in range(2)]
    fetched = lax.ppermute(partial, ("zh", "c"), split_pairs)
    near = lax.ppermute(partial, "zh", [(z, z ^ 1) for z in range(4)])
    partials = [partial, fetched, shift(fetched, "c", 2, 1), near]
    (frame_out,) = call(
        virtual_kernel, [((count, width), BF)], query, *partials, mine, virt_out, self_qkv, self_out
    )
    pieces = [frame_out] + [None] * (frames - 1)
    for k in GATHER_STEPS:
        pairs = [(f * 2 + c, (f ^ (k + c)) * 2 + c) for f in range(frames) for c in range(2)]
        pieces[k] = lax.ppermute(frame_out, ("x", "zl", "c"), pairs)
    pieces[1] = lax.ppermute(frame_out, "zl", [(0, 1), (1, 0)])
    for k in GATHER_STEPS:
        pieces[k + 1] = shift(pieces[k], "c", 2, 1)
    (front,) = call(
        front_kernel, [((len(FIRST_PLACES) * tracks, width), BF)],
        query, *[pieces[place] for place in FIRST_PLACES], back_kv,
    )
    tracks_out, virtual_out = call(
        back_kernel,
        [((rows, width), BF), ((count * frames, width), BF)],
        updated, query, swap_part, swap, front, *pieces, back_kv, back_out,
    )
    return tracks_out.reshape(tokens.shape), virtual_out.reshape(virtual.shape)


def solution(mesh):
    fine = Mesh(mesh.devices.reshape(4, 4, 2, 2, 4), ("x", "zh", "zl", "c", "y"))
    tokens = P(TRACK_AXES, "y", None)
    virtual = P(None, "y", None)
    return jax.shard_map(
        on_device,
        mesh=fine,
        in_specs=(tokens, P(TRACK_AXES, "y"), virtual) + (P(),) * 10,
        out_specs=(tokens, virtual),
        check_vma=False,
    )
```

```python
import jax
import jax.numpy as jnp
from jax import lax
from jax.experimental import pallas as pl
from jax.experimental.pallas import tpu as pltpu
from jax.sharding import Mesh
from jax.sharding import PartitionSpec as P

HEADS = 8
TILE = 256
EPS = 1e-05
NEG = -1e30
LOG2E = 1.4426950408889634
GROUP = 4
STEPS = (2, 1, 3)
EARLY = 1
GATHER_STEPS = (4, 2, 6)
FIRST_PLACES = (0, 1, 6, 7)
MARK = 64.0
BF = jnp.bfloat16
F32 = jnp.float32
TRACK_AXES = ("x", "zh", "zl", "c")


def normalize(values):
    widened = values.astype(F32)
    center = jnp.mean(widened, -1, keepdims=True)
    shifted = widened - center
    return (shifted * lax.rsqrt(jnp.mean(shifted * shifted, -1, keepdims=True) + EPS)).astype(BF)


def matmul(a, b):
    return lax.dot_general(a, b, (((1,), (0,)), ((), ())), preferred_element_type=F32)


def matmul_t(a, b):
    return lax.dot_general(a, b, (((1,), (1,)), ((), ())), preferred_element_type=F32)


def iota(shape, dim):
    return lax.broadcasted_iota(jnp.int32, shape, dim)


def scale_of(width):
    return float((width // HEADS) ** (-0.5)) * LOG2E


def tile(rows, j):
    return rows[:, :TILE] if j == 0 else rows[:, rows.shape[1] - TILE :]


def tile_masks(width, j):
    each = width // HEADS
    lane = iota((1, TILE), 1) + j * (width - TILE)
    return [(lane >= h * each) & (lane < (h + 1) * each) for h in range(4 * j, 4 * j + 4)]


def stack_heads(rows, j):
    part = tile(rows, j)
    return jnp.concatenate(
        [part * mask.astype(F32).astype(rows.dtype) for mask in tile_masks(rows.shape[1], j)], axis=0
    )


def pick_heads(stacked, j, width):
    masks = tile_masks(width, j)
    count = stacked.shape[0] // 4
    total = stacked[:count]
    for k in range(1, 4):
        total = jnp.where(masks[k], stacked[k * count : (k + 1) * count], total)
    return total


def join_tiles(a, b, width):
    middle = jnp.where(iota((1, 128), 1) < width // 2 - 128, a[:, 128:], b[:, :128])
    return jnp.concatenate([a[:, :128], middle, b[:, 128:]], axis=1)


def attend(items, width):
    scale = scale_of(width)
    tiles = [(j, *item) for item in items for j in (0, 1)]
    scores = []
    for j, queries, keys, _, bias in tiles:
        raw = matmul_t(stack_heads(queries, j), tile(keys, j))
        if bias is not None:
            raw = (raw.reshape(4, queries.shape[0], -1) + bias).reshape(raw.shape)
        scores.append(raw)
    terms = [jnp.exp2((raw - jnp.max(raw, -1, keepdims=True)) * scale) for raw in scores]
    mixed = []
    for (j, _, _, values, _), term in zip(tiles, terms):
        share = 1.0 / jnp.sum(term, -1, keepdims=True)
        mixed.append(pick_heads(matmul(term.astype(BF), tile(values, j)) * share, j, width))
    return [join_tiles(a, b, width).astype(BF) for a, b in zip(mixed[::2], mixed[1::2])]


def swap_matrix(outer, inner):
    n = outer * inner
    row, col = iota((n, n), 0), iota((n, n), 1)
    source = (row & (inner - 1)) * outer + (row >> (inner.bit_length() - 1))
    return jnp.where(col == source, 1.0, 0.0).astype(BF)


def own_kernel(
    tokens_ref, virtual_ref, visible_ref, time_qkv_ref, virt_q_ref, qkv_ref, query_ref, by_frame_ref, seen_ref
):
    rows = tokens_ref.shape[0]
    tracks, frames = visible_ref.shape
    by_frame_ref[...] = swap_matrix(frames, tracks)
    pick = jnp.where((iota((rows, tracks), 0) & (tracks - 1)) == iota((rows, tracks), 1), 1.0, 0.0).astype(BF)
    spread = matmul(pick, visible_ref[...].astype(F32).astype(BF))
    here = iota((rows, frames), 0) // tracks == iota((rows, frames), 1)
    seen = jnp.sum(jnp.where(here, spread, 0.0), -1, keepdims=True)
    seen_ref[...] = jnp.broadcast_to(seen, seen_ref.shape)
    qkv_ref[...] = matmul(normalize(tokens_ref[...]), time_qkv_ref[...]).astype(BF)
    query_ref[...] = matmul(normalize(virtual_ref[...]), virt_q_ref[...]).astype(BF)


def pair_kernel(tokens_ref, time_qkv_ref, out_ref):
    width = tokens_ref.shape[1]
    out_ref[...] = matmul(normalize(tokens_ref[...]), time_qkv_ref[:, width:]).astype(BF)


def time_kernel(
    frames, group, early, tokens_ref, qkv_ref, *refs
):
    piece_refs = refs[:3]
    by_frame_ref, seen_ref, time_qkv_ref, time_out_ref, updated_ref, send_ref, normed_ref = refs[3:]
    rows, width = tokens_ref.shape
    size = group * frames
    pairs = [qkv_ref[:, width:]] + [ref[...] for ref in piece_refs[:early]]
    pairs += [matmul(normalize(ref[...]), time_qkv_ref[:, width:]).astype(BF) for ref in piece_refs[early:]]
    row, col = iota((size, 4 * size), 0), iota((size, 4 * size), 1)
    bias = jnp.where(row // frames == (col & (size - 1)) // frames, 0.0, NEG)[None]
    items = []
    for start in range(0, rows, size):
        span = slice(start, start + size)
        keys = jnp.concatenate([pair[span, :width] for pair in pairs], axis=0)
        values = jnp.concatenate([pair[span, width:] for pair in pairs], axis=0)
        items.append((qkv_ref[span, :width], keys, values, bias))
    mixed = jnp.concatenate(attend(items, width), axis=0)
    updated = (tokens_ref[...].astype(F32) + matmul(mixed, time_out_ref[...])).astype(BF)
    updated_ref[...] = updated
    normed = matmul(by_frame_ref[...], normalize(updated))
    seen = seen_ref[:, :1] > 0.5
    send_ref[...] = jnp.where(seen, normed, MARK).astype(BF)
    normed_ref[...] = normed.astype(BF)


def split(value):
    high = value.astype(BF)
    rest = value - high.astype(F32)
    middle = rest.astype(BF)
    return [high, middle, (rest - middle.astype(F32)).astype(BF)]


def pack_stats(peak, total):
    lane = iota(peak.shape, 1)
    stats = jnp.zeros(peak.shape, F32)
    for k, piece in enumerate(split(peak) + split(total)):
        stats = jnp.where(lane >> 3 == k, piece.astype(F32), stats)
    return stats.astype(BF)


def partial_kernel(rows_ref, query_ref, virt_kv_ref, out_ref):
    rows = rows_ref[...]
    width = rows.shape[1]
    count = query_ref.shape[0]
    scale = scale_of(width)
    pair = matmul(rows, virt_kv_ref[...]).astype(BF)
    first = jnp.where(iota((8, width), 1) == 0, 1.0, 0.0).astype(BF)
    bias = jnp.where(matmul_t(first, rows)[:1] < MARK / 2, 0.0, NEG)
    scores = [matmul_t(stack_heads(query_ref[...], j), tile(pair[:, :width], j)) + bias for j in (0, 1)]
    peaks = [jnp.max(raw, -1, keepdims=True) for raw in scores]
    terms = [jnp.exp2((raw - peak) * scale) for raw, peak in zip(scores, peaks)]
    sums = [jnp.sum(term, -1, keepdims=True) for term in terms]
    mixed = [
        pick_heads(matmul(term.astype(BF), tile(pair[:, width:], j)), j, width) for j, term in enumerate(terms)
    ]
    out_ref[:, :width] = join_tiles(*mixed, width).astype(BF)
    lane = iota((count, 128), 1)
    peak, total = jnp.zeros((count, 128), F32), jnp.zeros((count, 128), F32)
    for h in range(HEADS):
        span = slice(h % 4 * count, (h % 4 + 1) * count)
        peak = jnp.where((lane & 7) == h, peaks[h // 4][span], peak)
        total = jnp.where((lane & 7) == h, sums[h // 4][span], total)
    out_ref[:, width:] = pack_stats(peak, total)


def merge(parts, width):
    scale = scale_of(width)
    each = width // HEADS
    lane, column = iota((128, width), 0), iota((128, width), 1)
    mine = (column >= (lane & 7) * each) & (column < ((lane & 7) + 1) * each)
    spread_peak = jnp.where(mine & (lane < 24), 1.0, 0.0).astype(BF)
    spread_sum = jnp.where(mine & (lane >= 24) & (lane < 48), 1.0, 0.0).astype(BF)
    peaks = [matmul(part[:, width:], spread_peak) for part in parts]
    sums = [matmul(part[:, width:], spread_sum) for part in parts]
    top = peaks[0]
    for peak in peaks[1:]:
        top = jnp.maximum(top, peak)
    weighted, denominator = 0.0, 0.0
    for part, peak, total in zip(parts, peaks, sums):
        weight = jnp.exp2((peak - top) * scale)
        weighted = weighted + weight * part[:, :width].astype(F32)
        denominator = denominator + weight * total
    return (weighted / denominator).astype(BF)


def both_kernel(a_ref, b_ref, out_ref):
    width = a_ref.shape[1] - 128
    scale = scale_of(width)
    each = width // HEADS
    source, lane = iota((128, 256), 0), iota((128, 256), 1)
    same = (source & 7) == (lane & 7)
    here = ((lane < 128) & (source < 24)) | ((lane >= 128) & (source >= 24) & (source < 48))
    gather = jnp.where(same & here, 1.0, 0.0).astype(BF)
    parts = [a_ref[...], b_ref[...]]
    stats = [matmul(part[:, width:], gather) for part in parts]
    peaks, sums = [s[:, :128] for s in stats], [s[:, 128:] for s in stats]
    top = jnp.maximum(*peaks)
    weights = [jnp.exp2((peak - top) * scale) for peak in peaks]
    lane, column = iota((128, width), 0), iota((128, width), 1)
    spread = jnp.where(
        (column >= (lane & 7) * each) & (column < ((lane & 7) + 1) * each) & (lane < 16), 1.0, 0.0
    ).astype(BF)
    total, mixed = 0.0, 0.0
    for part, weight, count in zip(parts, weights, sums):
        high = weight.astype(BF)
        low = weight - high.astype(F32)
        pieces = jnp.where(iota(weight.shape, 1) < 8, high.astype(F32), low).astype(BF)
        mixed = mixed + matmul(pieces, spread) * part[:, :width].astype(F32)
        total = total + weight * count
    out_ref[:, :width] = mixed.astype(BF)
    out_ref[:, width:] = pack_stats(top, total)


def virtual_kernel(*refs):
    _, *part_refs, virtual_ref, virt_out_ref, self_qkv_ref, self_out_ref, out_ref = refs
    width = virtual_ref.shape[1]
    attended = merge([ref[...] for ref in part_refs], width)
    cross = (virtual_ref[...].astype(F32) + matmul(attended, virt_out_ref[...])).astype(BF)
    proj = matmul(normalize(cross), self_qkv_ref[...]).astype(BF)
    (mixed,) = attend([(proj[:, :width], proj[:, width : 2 * width], proj[:, 2 * width :], None)], width)
    out_ref[...] = (cross.astype(F32) + matmul(mixed, self_out_ref[...])).astype(BF)


def query_kernel(place_ref, normed_ref, back_q_ref, out_ref, swap_part_ref, swap_ref):
    frame, core = place_ref[0], place_ref[1]
    rows = normed_ref.shape[0]
    frames = 8
    tracks = rows // frames

    def turn(place):
        return jnp.where(place >= 2, place ^ core, place)

    def swap(n):
        row, col = iota((n, n), 0), iota((n, n), 1)
        source = turn((row & (frames - 1)) ^ frame) * (n // frames) + (row >> (frames.bit_length() - 1))
        return jnp.where(col == source, 1.0, 0.0).astype(BF)

    swap_part_ref[...] = swap(swap_part_ref.shape[0])
    swap_ref[...] = swap(rows)
    starts = [pl.multiple_of((turn(jnp.int32(place)) ^ frame) * tracks, tracks) for place in range(frames)]
    ordered = jnp.concatenate([normed_ref[pl.ds(start, tracks)] for start in starts], axis=0)
    out_ref[...] = matmul(ordered, back_q_ref[...]).astype(BF)


def attend_pieces(places, tracks, query_ref, piece_refs, back_kv_ref):
    count, width = piece_refs[0].shape
    flat = jnp.concatenate([ref[...] for ref in piece_refs], axis=0)
    pair = matmul(normalize(flat), back_kv_ref[...]).astype(BF)
    items = []
    for k, place in enumerate(places):
        span = slice(k * count, (k + 1) * count)
        queries = query_ref[place * tracks : (place + 1) * tracks]
        items.append((queries, pair[span, :width], pair[span, width:], None))
    return attend(items, width)


def front_kernel(query_ref, *refs):
    *piece_refs, back_kv_ref, out_ref = refs
    tracks = out_ref.shape[0] // len(FIRST_PLACES)
    out_ref[...] = jnp.concatenate(
        attend_pieces(FIRST_PLACES, tracks, query_ref, piece_refs, back_kv_ref), axis=0
    )


def back_kernel(updated_ref, query_ref, swap_part_ref, swap_ref, front_ref, *refs):
    *piece_refs, back_kv_ref, back_out_ref, out_ref, virtual_out_ref = refs
    frames = len(piece_refs)
    count = piece_refs[0].shape[0]
    tracks = updated_ref.shape[0] // frames
    step = swap_part_ref.shape[0] // frames
    for start in range(0, count, step):
        block = jnp.concatenate([ref[start : start + step] for ref in piece_refs], axis=0)
        virtual_out_ref[start * frames : (start + step) * frames] = matmul(swap_part_ref[...], block).astype(BF)
    rest = [place for place in range(frames) if place not in FIRST_PLACES]
    mixed = dict(zip(rest, attend_pieces(rest, tracks, query_ref, [piece_refs[k] for k in rest], back_kv_ref)))
    for k, place in enumerate(FIRST_PLACES):
        mixed[place] = front_ref[k * tracks : (k + 1) * tracks]
    mixed = jnp.concatenate([mixed[place] for place in range(frames)], axis=0)
    by_track = matmul(swap_ref[...], mixed).astype(BF)
    out_ref[...] = (updated_ref[...].astype(F32) + matmul(by_track, back_out_ref[...])).astype(BF)


def call(kernel, outs, *args, megabytes=32):
    spaces = [pltpu.SMEM if arg.dtype == jnp.int32 and arg.ndim == 1 else pltpu.VMEM for arg in args]
    return pl.pallas_call(
        kernel,
        out_shape=[jax.ShapeDtypeStruct(shape, dtype) for shape, dtype in outs],
        in_specs=[pl.BlockSpec(memory_space=space) for space in spaces],
        compiler_params=pltpu.CompilerParams(vmem_limit_bytes=megabytes * 1024 * 1024),
    )(*args)


def shift(value, axis, count, step):
    return lax.ppermute(value, axis, [(i, (i + step) % count) for i in range(count)])


def on_device(
    tokens, visible, virtual, time_qkv, time_out, virt_q, virt_kv, virt_out, self_qkv, self_out, back_q, back_kv,
    back_out,
):
    tracks, frames, width = tokens.shape
    count = virtual.shape[0]
    rows = tracks * frames
    flat = tokens.reshape(rows, width)
    others = [shift(flat, "y", 4, step) for step in STEPS]
    frame = lax.axis_index("x") * 2 + lax.axis_index("zl")
    mine = lax.dynamic_slice_in_dim(virtual, frame, 1, axis=1).reshape(count, width)
    qkv, virt_query, by_frame, seen = call(
        own_kernel,
        [((rows, 3 * width), BF), ((count, width), BF), ((rows, rows), BF), ((rows, 128), F32)],
        flat, mine, visible, time_qkv, virt_q,
    )
    for k in range(EARLY):
        (others[k],) = call(pair_kernel, [((rows, 2 * width), BF)], others[k], time_qkv)
    updated, send, normed = call(
        lambda *refs: time_kernel(frames, GROUP, EARLY, *refs),
        [((rows, width), BF)] * 3,
        flat, qkv, *others, by_frame, seen, time_qkv, time_out,
    )
    got = lax.all_to_all(send.reshape(frames, tracks, width), ("x", "zl"), 0, 0).reshape(rows, width)
    (partial,) = call(partial_kernel, [((count, width + 128), BF)], got, virt_query, virt_kv)
    (partial,) = call(both_kernel, [((count, width + 128), BF)], partial, shift(partial, "c", 2, 1))
    place = jnp.stack([frame, lax.axis_index("c")]).astype(jnp.int32)
    query, swap_part, swap = call(
        query_kernel, [((rows, width), BF), ((2 * count, 2 * count), BF), ((rows, rows), BF)], place, normed, back_q
    )
    split_pairs = [(z * 2 + c, (z ^ (2, 3)[c]) * 2 + c) for z in range(4) for c in range(2)]
    fetched = lax.ppermute(partial, ("zh", "c"), split_pairs)
    near = lax.ppermute(partial, "zh", [(z, z ^ 1) for z in range(4)])
    partials = [partial, fetched, shift(fetched, "c", 2, 1), near]
    (frame_out,) = call(
        virtual_kernel, [((count, width), BF)], query, *partials, mine, virt_out, self_qkv, self_out
    )
    pieces = [frame_out] + [None] * (frames - 1)
    for k in GATHER_STEPS:
        pairs = [(f * 2 + c, (f ^ (k + c)) * 2 + c) for f in range(frames) for c in range(2)]
        pieces[k] = lax.ppermute(frame_out, ("x", "zl", "c"), pairs)
    pieces[1] = lax.ppermute(frame_out, "zl", [(0, 1), (1, 0)])
    for k in GATHER_STEPS:
        pieces[k + 1] = shift(pieces[k], "c", 2, 1)
    (front,) = call(
        front_kernel, [((len(FIRST_PLACES) * tracks, width), BF)],
        query, *[pieces[place] for place in FIRST_PLACES], back_kv,
    )
    tracks_out, virtual_out = call(
        back_kernel,
        [((rows, width), BF), ((count * frames, width), BF)],
        updated, query, swap_part, swap, front, *pieces, back_kv, back_out,
    )
    return tracks_out.reshape(tokens.shape), virtual_out.reshape(virtual.shape)


def solution(mesh):
    fine = Mesh(mesh.devices.reshape(4, 4, 2, 2, 4), ("x", "zh", "zl", "c", "y"))
    tokens = P(TRACK_AXES, "y", None)
    virtual = P(None, "y", None)
    return jax.shard_map(
        on_device,
        mesh=fine,
        in_specs=(tokens, P(TRACK_AXES, "y"), virtual) + (P(),) * 10,
        out_specs=(tokens, virtual),
        check_vma=False,
    )
```
